128 devices in a mesh: dp: 4 (over y_hi, core), wide: 32 (over z, x, y_lo).
Axes of the slice: x: 4, y: 4 (y_hi: 2, y_lo: 2; y = y_hi * 2 + y_lo), z: 4, core: 2. Of those that a mesh axis runs over, the one named last changes fastest.
Arguments:
- frames: bfloat16 [4, 2, 64, 64, 512], P('dp', None, 'wide'), may hold values from -6 to 6
- conv_weight: bfloat16 [3, 512, 512], replicated, may hold values from -0.15625 to 0.15625
- embed_weight: bfloat16 [512, 1536], replicated, may hold values from -0.25 to 0.25
- query_weight: bfloat16 [1536, 1536], P('wide'), may hold values from -3 to 3
- key_weight: bfloat16 [1536, 1536], P('wide'), may hold values from -3 to 3
- value_weight: bfloat16 [1536, 1536], P('wide'), may hold values from -0.15625 to 0.15625
- output_weight: bfloat16 [1536, 1536], P('wide'), may hold values from -0.15625 to 0.15625
- out_grad: bfloat16 [4, 4, 64, 64, 1536], P('dp', None, 'wide'), may hold values from -0.119628906 to 0.119628906
- bucket_owner: int32 [16], replicated, may hold values from 0 to 3, as said below
- clip_bucket: int32 [4, 2], replicated, may hold values from 0 to 15, as said below
- clip_frames: int32 [4, 2], replicated, may hold values from 16 to 64, as said below
- clip_grid: int32 [4, 2, 2], replicated, may hold values from 2 to 32, as said below
Outputs:
- block_out: bfloat16 [4, 4, 64, 64, 1536], P('dp', None, 'wide')
- grad_query: float32 [1536, 1536], P('wide')
- grad_key: float32 [1536, 1536], P('wide')
- grad_value: float32 [1536, 1536], P('wide')
- grad_output: float32 [1536, 1536], P('wide')
The draws below stay inside these ranges and needn't reach their ends.
Inputs may be any that keep to these rules, and one draw needn't show every extreme that they name: `bucket_owner`: each owner has exactly 4 buckets. `clip_bucket`: the 2 clips of one group have buckets of different owners; some owner has a clip of every group. `clip_frames`: some clip has all 64 frames. `clip_grid`: the product of a clip's two entries is at most 64, and equals it for some clip.
All inputs are finite; a program needn't handle non-finite values.
Results may differ from the reference program's by a relative error of at most 0.025.
Values may be sent and summed in bfloat16 or wider, within the bound.
No kernel may reach another device: no remote copies, remote signals or barrier semaphores. Data moves between devices by JAX's collectives and lax.ppermute only.
A program may use at most 128 MiB of HBM per device.

```python
import math
import jax
import jax.numpy as jnp
from jax import lax

D = 1536
HEADS = 12
HEAD_DIM = 128
CHANNELS = 512
SITES = 64
FR_DEV = 2
CLIPS = 2
OWNER_BUCKETS = 4
TIME = 64
BUCKETS = 16
N_DP = 4
N_WIDE = 32


def bucket_plan(key):
    base = jax.random.fold_in(key, 11)
    order = jax.random.permutation(jax.random.fold_in(base, 1), BUCKETS)
    owners = order % N_DP
    inverse = jnp.argsort(order)
    last_code = order[BUCKETS - 1]
    anchor = last_code % N_DP
    last_pick = last_code // N_DP

    def one_group(group):
        group_key = jax.random.fold_in(base, 100 + group)
        others = (anchor + 1 + jax.random.permutation(jax.random.fold_in(group_key, 1), N_DP - 1)) % N_DP
        chosen = jnp.concatenate([anchor[None], others])[:CLIPS]
        picked = jax.random.randint(jax.random.fold_in(group_key, 3), (CLIPS,), 0, OWNER_BUCKETS)
        first_pick = jnp.where(group == 0, last_pick, picked[0])
        picked = jnp.concatenate([first_pick[None], picked[1:]])
        buckets = inverse[chosen + N_DP * picked]
        return jax.random.permutation(jax.random.fold_in(group_key, 2), buckets)
    buckets = jax.vmap(one_group)(jnp.arange(N_DP))
    return (owners.astype(jnp.int32), buckets.astype(jnp.int32))


def draw_bucket_owner(key, part):
    return bucket_plan(key)[0]


def draw_clip_bucket(key, part):
    return bucket_plan(key)[1]


def draw_clip_frames(key, part):
    base = jax.random.fold_in(key, 31)
    counts = jax.random.randint(jax.random.fold_in(base, 1), (N_DP * CLIPS,), TIME // 4, TIME + 1)
    chosen = jax.random.randint(jax.random.fold_in(base, 2), (), 0, N_DP * CLIPS)
    counts = jnp.where(jnp.arange(N_DP * CLIPS) == chosen, TIME, counts)
    return counts.reshape(N_DP, CLIPS).astype(jnp.int32)


def draw_clip_grid(key, part):
    base = jax.random.fold_in(key, 37)
    grid_rows = jax.random.randint(jax.random.fold_in(base, 1), (N_DP * CLIPS,), 2, 9)
    trimmed = jax.random.randint(jax.random.fold_in(base, 2), (N_DP * CLIPS,), 0, 2)
    order = jax.random.permutation(jax.random.fold_in(base, 3), N_DP * CLIPS)
    position = jnp.arange(N_DP * CLIPS)
    full_mark = position == order[0]
    tall_mark = position == order[1]
    narrow_mark = position == order[2]
    grid_rows = jnp.where(full_mark, 8, grid_rows)
    trimmed = jnp.where(full_mark, 0, trimmed)
    grid_rows = jnp.where(tall_mark, 2, grid_rows)
    trimmed = jnp.where(tall_mark, 0, trimmed)
    grid_rows = jnp.where(narrow_mark, 8, grid_rows)
    trimmed = jnp.where(narrow_mark, 1, trimmed)
    grid_cols = SITES // grid_rows - trimmed
    return jnp.stack([grid_rows, grid_cols], axis=-1).reshape(N_DP, CLIPS, 2).astype(jnp.int32)


def query_key_base(key):
    base = jax.random.fold_in(key, 47)
    shape = (D, HEADS * HEAD_DIM)
    shared = jnp.clip(jax.random.normal(jax.random.fold_in(base, 1), shape, jnp.float32), -4.0, 4.0)
    other = jnp.clip(jax.random.normal(jax.random.fold_in(base, 2), shape, jnp.float32), -4.0, 4.0)
    return (shared, other)


def draw_query_weight(key, part):
    shared, other = query_key_base(key)
    values = shared
    return (values / math.sqrt(D)).astype(jnp.bfloat16)


def draw_key_weight(key, part):
    shared, other = query_key_base(key)
    values = other
    return (values / math.sqrt(D)).astype(jnp.bfloat16)


def block_levels(own_key, dims, pieces, low, high):
    loudness = 1.0
    for dim, parts in pieces:
        heights = jax.random.uniform(jax.random.fold_in(jax.random.fold_in(own_key, 6), dim), (parts,), jnp.float32, low / len(pieces), high / len(pieces))
        loudness = loudness * jnp.repeat(jnp.exp(heights), dims[dim] // parts).reshape((-1,) + (1,) * (len(dims) - 1 - dim))
    return loudness


def gaussian(rng, shape, scale, bound, cuts=(), kind=jnp.bfloat16):
    result = jax.random.normal(rng, shape, jnp.float32) * scale
    if len(cuts) > 0:
        result = block_levels(rng, shape, cuts, -0.22, 0.18) * result
    return jnp.clip(result, min=-bound, max=bound).astype(kind)


def setup_inputs(seed: int = 0) -> dict:
    key_list = jax.random.split(jax.random.key(seed), 13)
    frames = gaussian(key_list[0], (N_DP, CLIPS, TIME, SITES, CHANNELS), 1.0, 6.0, ((0, 4), (2, 32)))
    conv_weight = gaussian(key_list[1], (3, CHANNELS, CHANNELS), (3 * CHANNELS) ** -0.5, 0.15625)
    embed_weight = gaussian(key_list[2], (CHANNELS, D), CHANNELS ** -0.5, 0.25)
    query_weight = draw_query_weight(jax.random.fold_in(key_list[12], 71), 0)
    key_weight = draw_key_weight(jax.random.fold_in(key_list[12], 71), 0)
    value_weight = gaussian(key_list[5], (D, HEADS * HEAD_DIM), D ** -0.5, 0.15625, ((0, 32),))
    output_weight = gaussian(key_list[6], (HEADS * HEAD_DIM, D), (HEADS * HEAD_DIM) ** -0.5, 0.15625, ((0, 32),))
    out_grad = gaussian(key_list[7], (N_DP, N_DP, TIME, SITES, D), 0.02, 0.119628906, ((0, 4), (2, 32)))
    bucket_owner = draw_bucket_owner(jax.random.fold_in(key_list[12], 71), 0)
    clip_bucket = draw_clip_bucket(jax.random.fold_in(key_list[12], 71), 0)
    clip_frames = draw_clip_frames(jax.random.fold_in(key_list[12], 71), 0)
    clip_grid = draw_clip_grid(jax.random.fold_in(key_list[12], 71), 0)
    return {"frames": frames, "conv_weight": conv_weight, "embed_weight": embed_weight, "query_weight": query_weight, "key_weight": key_weight, "value_weight": value_weight, "output_weight": output_weight, "out_grad": out_grad, "bucket_owner": bucket_owner, "clip_bucket": clip_bucket, "clip_frames": clip_frames, "clip_grid": clip_grid}


EPS = 1e-06
masked_score = -1e+30

def widen(array):
    return lax.optimization_barrier(array).astype(jnp.float32)

def layer_norm(values):
    floats = values.astype(jnp.float32)
    center = floats - lax.optimization_barrier(jnp.mean(floats, axis=-1, keepdims=True))
    spread = lax.optimization_barrier(jnp.mean(center * center, axis=-1, keepdims=True))
    return (center * lax.rsqrt(spread + EPS)).astype(jnp.bfloat16)

def reference(frames, conv_weight, embed_weight, query_weight, key_weight, value_weight, output_weight, out_grad, bucket_owner, clip_bucket, clip_frames, clip_grid):
    scale = 1.0 / math.sqrt(HEAD_DIM)
    active = widen(jax.nn.silu(frames.astype(jnp.float32)).astype(jnp.bfloat16))
    summed = frames.astype(jnp.float32)
    for offset in range(3):
        moved = jnp.pad(active, ((0, 0), (0, 0), (offset, 0), (0, 0), (0, 0)))[:, :, :TIME]
        summed = summed + jnp.einsum('gctsa,ab->gctsb', moved, conv_weight[offset].astype(jnp.float32))
    encoded = summed.astype(jnp.bfloat16)
    embedded = jnp.einsum('gctsa,ad->gctsd', widen(encoded), embed_weight.astype(jnp.float32)).astype(jnp.bfloat16)
    owners = bucket_owner[clip_bucket]
    group_index = jnp.arange(N_DP, dtype=jnp.int32)
    table = (owners[None, :, :] == group_index[:, None, None]).astype(jnp.int32)
    grouped = jnp.einsum('ogc,gctsd->ogtsd', table.astype(jnp.float32), widen(embedded)).astype(jnp.bfloat16)
    live_frames = lax.optimization_barrier(jnp.sum(table * clip_frames[None], axis=-1))
    grid_tokens = clip_grid[..., 0] * clip_grid[..., 1]
    live_tokens = lax.optimization_barrier(jnp.sum(table * grid_tokens[None], axis=-1))
    key_tokens = jnp.where(live_tokens > 0, live_tokens, SITES)
    time_pos = jnp.arange(TIME, dtype=jnp.int32)
    site_pos = jnp.arange(SITES, dtype=jnp.int32)
    live = (time_pos[None, None, :, None] < live_frames[:, :, None, None]) & (site_pos[None, None, None, :] < live_tokens[:, :, None, None])
    normed = layer_norm(widen(grouped))
    head_shape = (N_DP, N_DP, TIME, SITES, HEADS, HEAD_DIM)
    query = jnp.einsum('ogtsd,de->ogtse', widen(normed), query_weight.astype(jnp.float32)).astype(jnp.bfloat16)
    keys = jnp.einsum('ogtsd,de->ogtse', widen(normed), key_weight.astype(jnp.float32)).astype(jnp.bfloat16)
    values = jnp.einsum('ogtsd,de->ogtse', widen(normed), value_weight.astype(jnp.float32)).astype(jnp.bfloat16)
    query_heads = query.reshape(head_shape)
    key_heads = keys.reshape(head_shape)
    value_heads = values.reshape(head_shape)
    scores = jnp.einsum('ogtshd,ogtuhd->ogthsu', widen(query_heads), widen(key_heads)) * scale
    key_mask = site_pos[None, None, :] < key_tokens[:, :, None]
    scores = jnp.where(key_mask[:, :, None, None, None, :], scores, masked_score)
    top = lax.optimization_barrier(jnp.max(scores, axis=-1, keepdims=True))
    weights = jnp.exp(scores - top)
    probs = weights / lax.optimization_barrier(jnp.sum(weights, axis=-1, keepdims=True))
    probs_low = probs.astype(jnp.bfloat16)
    attended = jnp.einsum('ogthsu,ogtuhd->ogtshd', widen(probs_low), widen(value_heads)).astype(jnp.bfloat16)
    attended = attended.reshape(N_DP, N_DP, TIME, SITES, D)
    projected = jnp.einsum('ogtsk,kd->ogtsd', widen(attended), output_weight.astype(jnp.float32))
    block = (widen(grouped) + projected).astype(jnp.bfloat16)
    block_out = jnp.where(live[..., None], block, jnp.zeros((), jnp.bfloat16))
    upstream = jnp.where(live[..., None], out_grad, jnp.zeros((), jnp.bfloat16))
    d_attended = jnp.einsum('ogtsd,kd->ogtsk', upstream.astype(jnp.float32), output_weight.astype(jnp.float32)).astype(jnp.bfloat16)
    d_att_heads = d_attended.reshape(head_shape)
    d_probs = jnp.einsum('ogtshd,ogtuhd->ogthsu', widen(d_att_heads), widen(value_heads))
    inner = lax.optimization_barrier(jnp.sum(probs * d_probs, axis=-1, keepdims=True))
    d_scores = (probs * (d_probs - inner) * scale).astype(jnp.bfloat16)
    d_query = jnp.einsum('ogthsu,ogtuhd->ogtshd', widen(d_scores), widen(key_heads)).astype(jnp.bfloat16).reshape(N_DP, N_DP, TIME, SITES, D)
    d_keys = jnp.einsum('ogthsu,ogtshd->ogtuhd', widen(d_scores), widen(query_heads)).astype(jnp.bfloat16).reshape(N_DP, N_DP, TIME, SITES, D)
    d_values = jnp.einsum('ogthsu,ogtshd->ogtuhd', widen(probs_low), widen(d_att_heads)).astype(jnp.bfloat16).reshape(N_DP, N_DP, TIME, SITES, D)
    pairs = ((normed, d_query), (normed, d_keys), (normed, d_values), (attended, upstream))
    zero_index = jnp.zeros((), jnp.int32)

    def add_block(running, index):
        owner_pos = index // N_WIDE
        slab_pos = index % N_WIDE * FR_DEV
        starts = (owner_pos, zero_index, slab_pos, zero_index, zero_index)
        updated = []
        for accum, pair in zip(running, pairs):
            left_rows = lax.dynamic_slice(pair[0], starts, (1, N_DP, FR_DEV, SITES, D)).reshape(-1, D)
            right_rows = lax.dynamic_slice(pair[1], starts, (1, N_DP, FR_DEV, SITES, D)).reshape(-1, D)
            term = jnp.dot(left_rows.T, right_rows, preferred_element_type=jnp.float32)
            updated.append(accum + widen(term.astype(jnp.bfloat16)))
        return (tuple(updated), None)
    empty = jnp.zeros((D, D), jnp.float32)
    totals, unused = lax.scan(add_block, (empty, empty, empty, empty), jnp.arange(N_DP * N_WIDE, dtype=jnp.int32))
    return (block_out, totals[0], totals[1], totals[2], totals[3])
```

```python
import math

import jax
import jax.numpy as jnp
from jax import lax
from jax.experimental import pallas as pl
from jax.experimental.pallas import tpu as pltpu
from jax.sharding import PartitionSpec as P

HEAD_DIM = 128
EPS = 1e-06
masked_score = -1e30

AXES = ("dp", "wide")
N_DEV = 128
N_WIDE = 32
HEAD_COLS = 384
ROWS = 48


def place_of(index):
    dp, wide = divmod(index, N_WIDE)
    y_hi, core = divmod(dp, 2)
    z, rest = divmod(wide, 8)
    x, y_lo = divmod(rest, 2)
    return core, x, y_hi * 2 + y_lo, z


def index_of(core, x, y, z):
    y_hi, y_lo = divmod(y % 4, 2)
    return (y_hi * 2 + core % 2) * N_WIDE + (z % 4) * 8 + (x % 4) * 2 + y_lo


def pairs_by(move):
    return [(i, index_of(*move(*place_of(i)))) for i in range(N_DEV)]


Y_PARTNER = pairs_by(lambda core, x, y, z: (core, x, y ^ 1, z))
CORE_PARTNER = pairs_by(lambda core, x, y, z: (core ^ 1, x, y, z))
Y_NEXT = pairs_by(lambda core, x, y, z: (core, x, y + 1, z))
Y_BEFORE = pairs_by(lambda core, x, y, z: (core, x, y - 1, z))
Y_ACROSS = pairs_by(lambda core, x, y, z: (core, x, y + 2, z))
DP_MOVES = [[(i, i ^ (k * N_WIDE)) for i in range(N_DEV)] for k in range(4)]
HALO = [(i, i + 1) for i in range(N_DEV) if (i + 1) % N_WIDE]


def output_source(core, x, y, z, flip):
    y_hi, y_lo = divmod(y, 2)
    return index_of(z // 2, x, y_hi * 2 + ((z % 2) ^ flip), 2 * y_lo + core)


OUT_PAIRS = [[(output_source(*place_of(i), flip), i) for i in range(N_DEV)] for flip in (0, 1)]
OUT_BACK = [[(b, a) for a, b in pairs] for pairs in OUT_PAIRS]


def rings(axis_of_core):
    groups = []
    for core in range(2):
        for a in range(4):
            for y in range(4):
                if axis_of_core[core] == "z":
                    groups.append([index_of(core, a, y, z) for z in range(4)])
                else:
                    groups.append([index_of(core, x, y, a) for x in range(4)])
    return groups


RINGS_FIRST = rings("xz")
RINGS_SECOND = rings("zx")
RINGS_X = rings("xx")


def send(array, pairs):
    return lax.ppermute(array, AXES, pairs)


def exchange(array, groups):
    return lax.all_to_all(array, AXES, 0, 0, tiled=True, axis_index_groups=groups)


def gather(array, groups):
    return exchange(jnp.broadcast_to(array[None], (4,) + array.shape), groups)


def in_order(bit, mine, other, axis=0):
    return jnp.stack([jnp.where(bit == 0, mine, other), jnp.where(bit == 0, other, mine)], axis)


def layer_norm(values):
    floats = values.astype(jnp.float32)
    center = floats - jnp.mean(floats, axis=-1, keepdims=True)
    spread = jnp.mean(center * center, axis=-1, keepdims=True)
    return (center * lax.rsqrt(spread + EPS)).astype(jnp.bfloat16)


def dot(a, b, dims=((1,), (0,))):
    return lax.dot_general(a, b, (dims, ((), ())), preferred_element_type=jnp.float32)


def attention_kernel(limit_ref, qkv_ref, d_att_ref, att_ref, grads_ref):
    rows = qkv_ref.shape[0]
    sites = rows // 2
    scale = 1.0 / math.sqrt(HEAD_DIM)
    limit = limit_ref[pl.program_id(0)]
    row = lax.broadcasted_iota(jnp.int32, (rows, rows), 0)
    col = lax.broadcasted_iota(jnp.int32, (rows, rows), 1)
    upper = col >= sites
    site = jnp.where(upper, col - sites, col)
    mask = (upper == (row >= sites)) & (site < limit)
    for head in range(HEAD_COLS // HEAD_DIM):
        at = head * HEAD_DIM
        cols = slice(at, at + HEAD_DIM)
        query = qkv_ref[:, cols]
        keys = qkv_ref[:, HEAD_COLS + at : HEAD_COLS + at + HEAD_DIM]
        values = qkv_ref[:, 2 * HEAD_COLS + at : 2 * HEAD_COLS + at + HEAD_DIM]
        d_att = d_att_ref[:, cols]
        scores = jnp.where(mask, dot(query, keys, ((1,), (1,))) * scale, masked_score)
        weights = jnp.exp(scores - jnp.max(scores, axis=-1, keepdims=True))
        probs = weights / jnp.sum(weights, axis=-1, keepdims=True)
        probs_low = probs.astype(jnp.bfloat16)
        att_ref[:, cols] = dot(probs_low, values).astype(jnp.bfloat16)
        d_probs = dot(d_att, values, ((1,), (1,)))
        inner = jnp.sum(probs * d_probs, axis=-1, keepdims=True)
        d_scores = (probs * (d_probs - inner) * scale).astype(jnp.bfloat16)
        grads_ref[:, cols] = dot(d_scores, keys).astype(jnp.bfloat16)
        grads_ref[:, HEAD_COLS + at : HEAD_COLS + at + HEAD_DIM] = dot(
            d_scores, query, ((0,), (0,))
        ).astype(jnp.bfloat16)
        grads_ref[:, 2 * HEAD_COLS + at : 2 * HEAD_COLS + at + HEAD_DIM] = dot(
            probs_low, d_att, ((0,), (0,))
        ).astype(jnp.bfloat16)


def attention(limits, qkv, d_att):
    rows = 128
    count = qkv.shape[0] // rows
    spec = lambda width: pl.BlockSpec((rows, width), lambda i, limits: (i, 0))
    return pl.pallas_call(
        attention_kernel,
        grid_spec=pltpu.PrefetchScalarGridSpec(
            num_scalar_prefetch=1,
            grid=(count,),
            in_specs=[spec(3 * HEAD_COLS), spec(HEAD_COLS)],
            out_specs=[spec(HEAD_COLS), spec(3 * HEAD_COLS)],
        ),
        out_shape=[
            jax.ShapeDtypeStruct((qkv.shape[0], HEAD_COLS), jnp.bfloat16),
            jax.ShapeDtypeStruct((qkv.shape[0], 3 * HEAD_COLS), jnp.bfloat16),
        ],
        compiler_params=pltpu.CompilerParams(vmem_limit_bytes=32 * 1024 * 1024),
        cost_estimate=pl.CostEstimate(
            flops=14 * count * 3 * rows * rows * HEAD_DIM,
            bytes_accessed=16 * qkv.shape[0] * HEAD_COLS,
            transcendentals=3 * count * rows * rows,
        ),
    )(limits, qkv, d_att)


def body(
    frames,
    conv_weight,
    embed_weight,
    query_weight,
    key_weight,
    value_weight,
    output_weight,
    out_grad,
    bucket_owner,
    clip_bucket,
    clip_frames,
    clip_grid,
):
    my_dp = lax.axis_index("dp")
    my_slab = lax.axis_index("wide")
    core, y_hi = my_dp % 2, my_dp // 2
    y_lo = my_slab % 2
    z_low = (my_slab // 8) % 2
    heads_now = 2 * y_lo + core
    heads_across = 2 * (1 - y_lo) + core
    frame_slab = frames[0]
    clip_count, slab_frames, site_count, channels = frame_slab.shape
    width = embed_weight.shape[1]
    own_rows = clip_count * slab_frames * site_count

    def head_columns(which):
        return jnp.concatenate(
            [
                lax.dynamic_slice(w, (0, which * HEAD_COLS), (ROWS, HEAD_COLS))
                for w in (query_weight, key_weight, value_weight)
            ],
            axis=1,
        )

    pair = in_order(y_lo, head_columns(heads_now), send(head_columns(heads_across), Y_PARTNER))
    ring = gather(pair, RINGS_FIRST)
    qkv_weight = gather(ring, RINGS_SECOND).reshape(width, 3 * HEAD_COLS)
    out_pair = in_order(
        z_low, send(output_weight, OUT_PAIRS[0]), send(output_weight, OUT_PAIRS[1])
    )
    out_rows = gather(out_pair, RINGS_X).reshape(HEAD_COLS, width)

    owners = bucket_owner[clip_bucket]
    tokens = clip_grid[..., 0] * clip_grid[..., 1]
    my_owners = owners[my_dp]
    frame_pos = my_slab * slab_frames + jnp.arange(slab_frames, dtype=jnp.int32)
    site_pos = jnp.arange(site_count, dtype=jnp.int32)
    live = (frame_pos[None, :, None] < clip_frames[my_dp][:, None, None]) & (
        site_pos[None, None, :] < tokens[my_dp][:, None, None]
    )
    group_tokens = lax.dynamic_slice(tokens, (2 * y_hi, 0), (2, clip_count)).reshape(-1)
    limits = jnp.concatenate([group_tokens, group_tokens])

    def to_group(own):
        both = in_order(y_lo, own, send(own, Y_PARTNER))
        return in_order(core, both, send(both, CORE_PARTNER), axis=1).reshape(-1, own.shape[-1])

    earlier = send(frame_slab, HALO)
    joined = jnp.concatenate([earlier, frame_slab], axis=1)
    active = jax.nn.silu(joined.astype(jnp.float32)).astype(jnp.bfloat16)
    summed = frame_slab.astype(jnp.float32).reshape(-1, channels)
    for offset in range(3):
        moved = active[:, slab_frames - offset : 2 * slab_frames - offset].reshape(-1, channels)
        summed = summed + dot(moved, conv_weight[offset])
    encoded = summed.astype(jnp.bfloat16)
    own_grouped = dot(encoded, embed_weight).astype(jnp.bfloat16)
    swapped = embed_weight.reshape(channels, 4, 4, -1).swapaxes(1, 2).reshape(channels, width)
    embed_now = jnp.where(core == 0, embed_weight, swapped)
    normed = layer_norm(dot(to_group(encoded), embed_now).astype(jnp.bfloat16))

    grads = out_grad[0]
    from_owner = []
    for k in range(4):
        part = lax.dynamic_index_in_dim(grads, my_dp ^ k, 0, keepdims=False)
        from_owner.append(part if k == 0 else send(part, DP_MOVES[k]))
    clip_up = []
    for clip in range(clip_count):
        place = my_owners[clip] ^ my_dp
        low = jnp.where(place == 0, from_owner[0], from_owner[1])
        high = jnp.where(place == 2, from_owner[2], from_owner[3])
        clip_up.append(jnp.where(place < 2, low, high))
    own_up = jnp.where(live[..., None], jnp.stack(clip_up), jnp.zeros((), jnp.bfloat16))
    upstream = to_group(own_up.reshape(own_rows, width))

    qkv = dot(normed, qkv_weight).astype(jnp.bfloat16)
    d_attended = dot(upstream, out_rows, ((1,), (1,))).astype(jnp.bfloat16)
    attended, d_qkv = attention(limits, qkv, d_attended)

    term_qkv = dot(normed, d_qkv, ((0,), (0,))).astype(jnp.bfloat16)
    term_out = dot(attended, upstream, ((0,), (0,))).astype(jnp.bfloat16)

    def reduced(array, groups):
        parts = exchange(array.reshape((4, -1) + array.shape[1:]), groups)
        return jnp.sum(parts.astype(jnp.float32), axis=0).astype(jnp.bfloat16)

    part_qkv = reduced(reduced(term_qkv, RINGS_SECOND), RINGS_FIRST).reshape(2, ROWS, -1)
    part_out = reduced(term_out, RINGS_X).reshape(2, ROWS, width)
    even = lax.dynamic_index_in_dim(part_out, z_low, 0, keepdims=False)
    odd = lax.dynamic_index_in_dim(part_out, 1 - z_low, 0, keepdims=False)
    mine_out = send(even, OUT_BACK[0]).astype(jnp.float32) + send(odd, OUT_BACK[1]).astype(
        jnp.float32
    )

    mine_qkv = lax.dynamic_index_in_dim(part_qkv, y_lo, 0, keepdims=False)
    other_qkv = lax.dynamic_index_in_dim(part_qkv, 1 - y_lo, 0, keepdims=False)
    across = send(jnp.concatenate([mine_qkv, mine_out.astype(jnp.bfloat16)], axis=1), Y_ACROSS)
    across = across.astype(jnp.float32)
    after = send(other_qkv, Y_NEXT).astype(jnp.float32)
    before = send(other_qkv, Y_BEFORE).astype(jnp.float32)
    same = mine_qkv.astype(jnp.float32) + across[:, : 3 * HEAD_COLS]
    cross = after + before
    total_out = mine_out + across[:, 3 * HEAD_COLS :]
    mine = jnp.concatenate([same, cross, total_out], axis=1)
    theirs = send(mine.astype(jnp.bfloat16), CORE_PARTNER).astype(jnp.float32)
    halves = in_order(core, mine[:, : 6 * HEAD_COLS], theirs[:, : 6 * HEAD_COLS])
    halves = halves.reshape(2, ROWS, 2, 3 * HEAD_COLS)
    low = jnp.where(y_lo == 0, halves[:, :, 0], halves[:, :, 1])
    high = jnp.where(y_lo == 0, halves[:, :, 1], halves[:, :, 0])
    pieces = (low[0], low[1], high[0], high[1])
    grad_query, grad_key, grad_value = (
        jnp.concatenate([p[:, i * HEAD_COLS : (i + 1) * HEAD_COLS] for p in pieces], axis=1)
        for i in range(3)
    )
    grad_output = mine[:, 6 * HEAD_COLS :] + theirs[:, 6 * HEAD_COLS :]

    partial = dot(attended, out_rows).astype(jnp.bfloat16).reshape(2, 2, own_rows, width)
    keep = lax.dynamic_index_in_dim(partial, core, 1, keepdims=False).astype(jnp.float32)
    give = lax.dynamic_index_in_dim(partial, 1 - core, 1, keepdims=False)
    chip = keep + send(give, CORE_PARTNER).astype(jnp.float32)
    keep = lax.dynamic_index_in_dim(chip, y_lo, 0, keepdims=False)
    give = lax.dynamic_index_in_dim(chip, 1 - y_lo, 0, keepdims=False).astype(jnp.bfloat16)
    projected = keep + send(give, Y_PARTNER).astype(jnp.float32)
    block = (own_grouped.astype(jnp.float32) + projected).astype(jnp.bfloat16)
    block = block.reshape(clip_count, slab_frames, site_count, width)
    block = jnp.where(live[..., None], block, jnp.zeros((), jnp.bfloat16))
    arrived = []
    for k in range(4):
        to_them = (my_owners ^ my_dp) == k
        part = jnp.where(
            to_them[0], block[0], jnp.where(to_them[1], block[1], jnp.zeros((), jnp.bfloat16))
        )
        arrived.append(part if k == 0 else send(part, DP_MOVES[k]))
    a0, a1, a2, a3 = arrived
    a0, a1 = jnp.where(core == 0, a0, a1), jnp.where(core == 0, a1, a0)
    a2, a3 = jnp.where(core == 0, a2, a3), jnp.where(core == 0, a3, a2)
    first, second = jnp.stack([a0, a1]), jnp.stack([a2, a3])
    block_out = in_order(y_hi, first, second).reshape(
        1, 4, slab_frames, site_count, width
    )
    return (block_out, grad_query, grad_key, grad_value, grad_output)


def solution(mesh):
    in_specs = (
        P("dp", None, "wide", None, None),
        P(),
        P(),
        P("wide", None),
        P("wide", None),
        P("wide", None),
        P("wide", None),
        P("dp", None, "wide", None, None),
        P(),
        P(),
        P(),
        P(),
    )
    out_specs = (
        P("dp", None, "wide", None, None),
        P("wide", None),
        P("wide", None),
        P("wide", None),
        P("wide", None),
    )
    return jax.shard_map(body, mesh=mesh, in_specs=in_specs, out_specs=out_specs, check_vma=False)
```

```python
import functools
import math

import jax
import jax.numpy as jnp
from jax import lax
from jax.experimental import pallas as pl
from jax.experimental.pallas import tpu as pltpu
from jax.sharding import PartitionSpec as P

HEAD_DIM = 128
EPS = 1e-06
masked_score = -1e30

NO_COST = pl.CostEstimate(flops=0, bytes_accessed=0, transcendentals=0)

AXES = ("dp", "wide")
N_DEV = 128
N_WIDE = 32
HEAD_COLS = 384
UNIT_ROWS = 128
UNITS = 2
ROWS = 48


def place_of(index):
    dp, wide = divmod(index, N_WIDE)
    y_hi, core = divmod(dp, 2)
    z, rest = divmod(wide, 8)
    x, y_lo = divmod(rest, 2)
    return core, x, y_hi * 2 + y_lo, z


def index_of(core, x, y, z):
    y_hi, y_lo = divmod(y % 4, 2)
    return (y_hi * 2 + core % 2) * N_WIDE + (z % 4) * 8 + (x % 4) * 2 + y_lo


def pairs_by(move):
    return [(i, index_of(*move(*place_of(i)))) for i in range(N_DEV)]


Y_PARTNER = pairs_by(lambda core, x, y, z: (core, x, y ^ 1, z))
CORE_PARTNER = pairs_by(lambda core, x, y, z: (core ^ 1, x, y, z))
Y_NEXT = pairs_by(lambda core, x, y, z: (core, x, y + 1, z))
Y_BEFORE = pairs_by(lambda core, x, y, z: (core, x, y - 1, z))
Y_ACROSS = pairs_by(lambda core, x, y, z: (core, x, y + 2, z))
DP_MOVES = [[(i, i ^ (k * N_WIDE)) for i in range(N_DEV)] for k in range(4)]
HALO = [(i, i + 1) for i in range(N_DEV) if (i + 1) % N_WIDE]


def output_source(core, x, y, z, flip):
    y_hi, y_lo = divmod(y, 2)
    place, across = (z, x) if core else (x, z)
    return index_of(across // 2, place, y_hi * 2 + ((across % 2) ^ flip), 2 * y_lo + core)


RING_FLIPS = [
    pairs_by(lambda core, x, y, z, k=k: (core, x, y, z ^ k) if core else (core, x ^ k, y, z))
    for k in range(4)
]


OUT_PAIRS = [[(output_source(*place_of(i), flip), i) for i in range(N_DEV)] for flip in (0, 1)]
def spot(index):
    core, x, _, z = place_of(index)
    return z if core else x


def output_target(core, x, y, z, block):
    y_hi, y_lo = divmod(y, 2)
    place, column = (x, z) if core else (z, x)
    return index_of(column // 2, place, y_hi * 2 + block, 2 * y_lo + core)


OUT_BACK = [
    [(i, output_target(*place_of(i), block=(spot(i) % 2) ^ flip)) for i in range(N_DEV)]
    for flip in (0, 1)
]


def rings(axis_of_core):
    groups = []
    for core in range(2):
        for a in range(4):
            for y in range(4):
                if axis_of_core[core] == "z":
                    groups.append([index_of(core, a, y, z) for z in range(4)])
                else:
                    groups.append([index_of(core, x, y, a) for x in range(4)])
    return groups


RINGS_FIRST = rings("xz")
RINGS_SECOND = rings("zx")


def send(array, pairs):
    return lax.ppermute(array, AXES, pairs)


def exchange(array, groups):
    return lax.all_to_all(array, AXES, 0, 0, tiled=True, axis_index_groups=groups)


def spread(array):
    return jnp.broadcast_to(array[None], (4,) + array.shape)


def in_order(bit, mine, other, axis=0):
    return jnp.stack([jnp.where(bit == 0, mine, other), jnp.where(bit == 0, other, mine)], axis)


def after(value, *others):
    return lax.optimization_barrier((value,) + others)[0]


def layer_norm(values):
    floats = values.astype(jnp.float32)
    center = floats - jnp.mean(floats, axis=-1, keepdims=True)
    spread = jnp.mean(center * center, axis=-1, keepdims=True)
    return (center * lax.rsqrt(spread + EPS)).astype(jnp.bfloat16)


def dot(a, b, dims=((1,), (0,))):
    return lax.dot_general(a, b, (dims, ((), ())), preferred_element_type=jnp.float32)


def product_kernel(dims, a_ref, b_ref, *rest):
    product = dot(a_ref[...], b_ref[...], dims)
    if len(rest) == 2:
        product = product + rest[0][...].astype(jnp.float32)
    rest[-1][...] = product.astype(jnp.bfloat16)


def matmul(a, b, dims=(1, 0), tile=256, add=None):
    rows, depth = a.shape[1 - dims[0]], a.shape[dims[0]]
    columns = b.shape[1 - dims[1]]
    if dims[0]:
        a_spec = pl.BlockSpec((tile, depth), lambda i: (i, 0))
    else:
        a_spec = pl.BlockSpec((depth, tile), lambda i: (0, i))
    out_spec = pl.BlockSpec((tile, columns), lambda i: (i, 0))
    return pl.pallas_call(
        functools.partial(product_kernel, ((dims[0],), (dims[1],))),
        grid=(rows // tile,),
        in_specs=[a_spec, pl.BlockSpec(b.shape, lambda i: (0, 0))]
        + ([out_spec] if add is not None else []),
        out_specs=out_spec,
        out_shape=jax.ShapeDtypeStruct((rows, columns), jnp.bfloat16),
        compiler_params=pltpu.CompilerParams(vmem_limit_bytes=40 * 1024 * 1024),
        cost_estimate=NO_COST,
    )(*((a, b) if add is None else (a, b, add)))


def matmul_columns(a, b):
    rows, depth = a.shape
    return pl.pallas_call(
        functools.partial(product_kernel, ((1,), (0,))),
        grid=(3,),
        in_specs=[
            pl.BlockSpec((rows, depth), lambda i: (0, 0)),
            pl.BlockSpec((depth, HEAD_COLS), lambda i: (0, i)),
        ],
        out_specs=pl.BlockSpec((rows, HEAD_COLS), lambda i: (0, i)),
        out_shape=jax.ShapeDtypeStruct((rows, b.shape[1]), jnp.bfloat16),
        compiler_params=pltpu.CompilerParams(vmem_limit_bytes=40 * 1024 * 1024),
        cost_estimate=NO_COST,
    )(a, b)


def split_kernel(ring_ref, spread_ref, out_ref):
    spread_ref[0] = ring_ref[:, : 3 * HEAD_COLS]

    @pl.when(pl.program_id(0) == 0)
    def _():
        out_ref[...] = ring_ref[:, 3 * HEAD_COLS :]


def split_ring(ring):
    rows, width = ring.shape[0], ring.shape[1] - 3 * HEAD_COLS
    return pl.pallas_call(
        split_kernel,
        grid=(4,),
        in_specs=[pl.BlockSpec(ring.shape, lambda i: (0, 0))],
        out_specs=[
            pl.BlockSpec((1, rows, 3 * HEAD_COLS), lambda i: (i, 0, 0)),
            pl.BlockSpec((rows, width), lambda i: (0, 0)),
        ],
        out_shape=[
            pltpu.HBM((4, rows, 3 * HEAD_COLS), jnp.bfloat16),
            jax.ShapeDtypeStruct((rows, width), jnp.bfloat16),
        ],
        compiler_params=pltpu.CompilerParams(vmem_limit_bytes=32 * 1024 * 1024),
        cost_estimate=NO_COST,
    )(ring)


def term_kernel(normed_ref, d_qkv_ref, att_ref, up_ref, out_ref, total_ref):
    out_ref[0, :, : 3 * HEAD_COLS] = dot(
        normed_ref[...], d_qkv_ref[...], ((0,), (0,))
    ).astype(jnp.bfloat16)

    @pl.when(pl.program_id(0) == 0)
    def _():
        total_ref[...] = dot(att_ref[...], up_ref[...], ((0,), (0,))).astype(jnp.bfloat16)

    at = pl.multiple_of(pl.program_id(0) * 2 * ROWS, 2 * ROWS)
    for block in range(4):
        out_ref[0, block * 2 * ROWS : (block + 1) * 2 * ROWS, 3 * HEAD_COLS :] = total_ref[
            pl.ds(at, 2 * ROWS), block * HEAD_COLS : (block + 1) * HEAD_COLS
        ]


def terms(normed, d_qkv, attended, upstream):
    depth, width = normed.shape
    rows = width // 4
    whole = lambda array: pl.BlockSpec(array.shape, lambda i: (0, 0))
    return pl.pallas_call(
        term_kernel,
        grid=(4,),
        in_specs=[
            pl.BlockSpec((depth, rows), lambda i: (0, i)),
            whole(d_qkv),
            whole(attended),
            whole(upstream),
        ],
        out_specs=pl.BlockSpec((1, rows, 4 * HEAD_COLS), lambda i: (i, 0, 0)),
        out_shape=pltpu.HBM((4, rows, 4 * HEAD_COLS), jnp.bfloat16),
        scratch_shapes=[pltpu.VMEM((HEAD_COLS, width), jnp.bfloat16)],
        compiler_params=pltpu.CompilerParams(vmem_limit_bytes=40 * 1024 * 1024),
        cost_estimate=NO_COST,
    )(normed, d_qkv, attended, upstream)


def sum_kernel(parts_ref, out_ref):
    total = parts_ref[0].astype(jnp.float32)
    for i in range(1, 4):
        total = total + parts_ref[i].astype(jnp.float32)
    out_ref[...] = total.astype(jnp.bfloat16)


def sum_parts(parts):
    rows, width = parts.shape[1:]
    tile = 2 * ROWS if rows > 2 * ROWS else ROWS
    return pl.pallas_call(
        sum_kernel,
        grid=(rows // tile,),
        in_specs=[pl.BlockSpec((4, tile, width), lambda i: (0, i, 0))],
        out_specs=pl.BlockSpec((tile, width), lambda i: (i, 0)),
        out_shape=jax.ShapeDtypeStruct((rows, width), jnp.bfloat16),
        compiler_params=pltpu.CompilerParams(vmem_limit_bytes=32 * 1024 * 1024),
        cost_estimate=NO_COST,
    )(parts)


def final_kernel(place_ref, mine_ref, theirs_ref, query_ref, key_ref, value_ref, output_ref):
    core, y_lo = place_ref[0], place_ref[1]
    wide = 3 * HEAD_COLS
    for kind, out in enumerate((query_ref, key_ref, value_ref)):
        for step in range(2):
            at = step * wide + kind * HEAD_COLS
            mine = mine_ref[:, at : at + HEAD_COLS]
            theirs = theirs_ref[:, at : at + HEAD_COLS].astype(jnp.float32)
            low = jnp.where(core == 0, mine, theirs)
            high = jnp.where(core == 0, theirs, mine)
            for side in range(2):

                @pl.when((y_lo ^ step) == side)
                def _():
                    begin = 2 * side * HEAD_COLS
                    out[:, begin : begin + HEAD_COLS] = low
                    out[:, begin + HEAD_COLS : begin + 2 * HEAD_COLS] = high

    mine = mine_ref[:, 2 * wide :]
    theirs = theirs_ref[:, 2 * wide :].astype(jnp.float32)
    output_ref[:, : 2 * HEAD_COLS] = jnp.where(core == 0, mine, theirs)
    output_ref[:, 2 * HEAD_COLS :] = jnp.where(core == 0, theirs, mine)


def final_grads(core, y_lo, mine, theirs):
    rows, width = mine.shape[0], 4 * HEAD_COLS
    whole = pl.BlockSpec(memory_space=pltpu.VMEM)
    return pl.pallas_call(
        final_kernel,
        in_specs=[pl.BlockSpec(memory_space=pltpu.SMEM), whole, whole],
        out_specs=[whole] * 4,
        out_shape=[jax.ShapeDtypeStruct((rows, width), jnp.float32)] * 4,
        cost_estimate=NO_COST,
    )(jnp.stack([core, y_lo]).astype(jnp.int32), mine, theirs)


def attention_kernel(limit_ref, qkv_ref, d_att_ref, att_ref, grads_ref):
    rows = UNIT_ROWS
    sites = rows // 2
    scale = 1.0 / math.sqrt(HEAD_DIM)
    row = lax.broadcasted_iota(jnp.int32, (rows, rows), 0)
    col = lax.broadcasted_iota(jnp.int32, (rows, rows), 1)
    upper = col >= sites
    site = jnp.where(upper, col - sites, col)
    block = upper == (row >= sites)
    masks = [
        block & (site < limit_ref[pl.program_id(0) * UNITS + unit]) for unit in range(UNITS)
    ]
    units = [(unit, head) for unit in range(UNITS) for head in range(HEAD_COLS // HEAD_DIM)]

    def part(ref, unit, head, kind):
        return ref[
            unit * rows : (unit + 1) * rows,
            kind * HEAD_COLS + head * HEAD_DIM : kind * HEAD_COLS + (head + 1) * HEAD_DIM,
        ]

    def put(ref, unit, head, kind, value):
        ref[
            unit * rows : (unit + 1) * rows,
            kind * HEAD_COLS + head * HEAD_DIM : kind * HEAD_COLS + (head + 1) * HEAD_DIM,
        ] = value.astype(jnp.bfloat16)

    scores = [
        dot(part(qkv_ref, u, h, 0), part(qkv_ref, u, h, 1), ((1,), (1,))) for u, h in units
    ]
    d_probs = [
        dot(part(d_att_ref, u, h, 0), part(qkv_ref, u, h, 2), ((1,), (1,))) for u, h in units
    ]
    low = []
    d_scores = []
    for (u, h), score, d_prob in zip(units, scores, d_probs):
        score = jnp.where(masks[u], score * scale, masked_score)
        weights = jnp.exp(score - jnp.max(score, axis=-1, keepdims=True))
        probs = weights * (1.0 / jnp.sum(weights, axis=-1, keepdims=True))
        inner = jnp.sum(probs * d_prob, axis=-1, keepdims=True)
        low.append(probs.astype(jnp.bfloat16))
        d_scores.append((probs * (d_prob - inner) * scale).astype(jnp.bfloat16))
    for (u, h), prob, d_score in zip(units, low, d_scores):
        put(att_ref, u, h, 0, dot(prob, part(qkv_ref, u, h, 2)))
        put(grads_ref, u, h, 0, dot(d_score, part(qkv_ref, u, h, 1)))
        put(grads_ref, u, h, 1, dot(d_score, part(qkv_ref, u, h, 0), ((0,), (0,))))
        put(grads_ref, u, h, 2, dot(prob, part(d_att_ref, u, h, 0), ((0,), (0,))))


def attention(limits, qkv, d_att):
    rows = UNITS * UNIT_ROWS
    count = qkv.shape[0] // rows
    spec = lambda width: pl.BlockSpec((rows, width), lambda i, limits: (i, 0))
    return pl.pallas_call(
        attention_kernel,
        grid_spec=pltpu.PrefetchScalarGridSpec(
            num_scalar_prefetch=1,
            grid=(count,),
            in_specs=[spec(3 * HEAD_COLS), spec(HEAD_COLS)],
            out_specs=[spec(HEAD_COLS), spec(3 * HEAD_COLS)],
        ),
        out_shape=[
            jax.ShapeDtypeStruct((qkv.shape[0], HEAD_COLS), jnp.bfloat16),
            jax.ShapeDtypeStruct((qkv.shape[0], 3 * HEAD_COLS), jnp.bfloat16),
        ],
        compiler_params=pltpu.CompilerParams(vmem_limit_bytes=32 * 1024 * 1024),
        cost_estimate=NO_COST,
    )(limits, qkv, d_att)


def body(
    frames,
    conv_weight,
    embed_weight,
    query_weight,
    key_weight,
    value_weight,
    output_weight,
    out_grad,
    bucket_owner,
    clip_bucket,
    clip_frames,
    clip_grid,
):
    my_dp = lax.axis_index("dp")
    my_slab = lax.axis_index("wide")
    core, y_hi = my_dp % 2, my_dp // 2
    y_lo = my_slab % 2
    heads_now = 2 * y_lo + core
    heads_across = 2 * (1 - y_lo) + core
    frame_slab = frames[0]
    clip_count, slab_frames, site_count, channels = frame_slab.shape
    width = embed_weight.shape[1]
    own_rows = clip_count * slab_frames * site_count

    def head_columns(which):
        return jnp.concatenate(
            [
                lax.dynamic_slice(w, (0, which * HEAD_COLS), (ROWS, HEAD_COLS))
                for w in (query_weight, key_weight, value_weight)
            ],
            axis=1,
        )

    x_place, z_place = (my_slab // 2) % 4, my_slab // 8
    place = jnp.where(core == 0, x_place, z_place)
    across_place = jnp.where(core == 0, z_place, x_place)
    parity = across_place % 2

    outgoing = head_columns(heads_across)
    grads = after(out_grad[0], outgoing)
    pair = in_order(y_lo, head_columns(heads_now), send(outgoing, Y_PARTNER))
    out_pair = in_order(
        parity, send(output_weight, OUT_PAIRS[0]), send(output_weight, OUT_PAIRS[1])
    )
    first_operand = spread(jnp.concatenate([pair, out_pair], axis=2))
    embed_weight = after(embed_weight, first_operand)
    earlier = send(after(frame_slab, pair), HALO)
    bucket_owner, clip_bucket, clip_frames, clip_grid = lax.optimization_barrier(
        (bucket_owner, clip_bucket, clip_frames, clip_grid, earlier)
    )[:-1]
    ring = exchange(first_operand, RINGS_FIRST)
    owners = bucket_owner[clip_bucket]
    tokens = clip_grid[..., 0] * clip_grid[..., 1]
    my_owners = owners[my_dp]
    frame_pos = my_slab * slab_frames + jnp.arange(slab_frames, dtype=jnp.int32)
    site_pos = jnp.arange(site_count, dtype=jnp.int32)
    live = (frame_pos[None, :, None] < clip_frames[my_dp][:, None, None]) & (
        site_pos[None, None, :] < tokens[my_dp][:, None, None]
    )
    group_tokens = lax.dynamic_slice(tokens, (2 * y_hi, 0), (2, clip_count)).reshape(-1)
    limits = jnp.concatenate([group_tokens, group_tokens])

    def to_group(own, *others):
        both = in_order(y_lo, own, after(send(own, Y_PARTNER), *others))
        return in_order(core, both, send(both, CORE_PARTNER), axis=1).reshape(-1, own.shape[-1])

    joined = jnp.concatenate([earlier, frame_slab], axis=1)
    active = jax.nn.silu(joined.astype(jnp.float32)).astype(jnp.bfloat16)
    summed = frame_slab.astype(jnp.float32).reshape(-1, channels)
    for offset in range(3):
        moved = active[:, slab_frames - offset : 2 * slab_frames - offset].reshape(-1, channels)
        summed = summed + dot(moved, conv_weight[offset])
    encoded = summed.astype(jnp.bfloat16)
    own_grouped = dot(encoded, embed_weight).astype(jnp.bfloat16)
    swapped = embed_weight.reshape(channels, 4, 4, -1).swapaxes(1, 2).reshape(channels, width)
    embed_now = jnp.where(core == 0, embed_weight, swapped)

    flips = [my_owners[clip] ^ my_dp for clip in range(clip_count)]
    from_owner = []
    for k in range(4):
        part = lax.dynamic_index_in_dim(grads, my_dp ^ k, 0, keepdims=False)
        part = after(part, first_operand) if k == 1 else part
        from_owner.append(part if k == 0 else send(part, DP_MOVES[k]))
    clip_up = []
    for clip in range(clip_count):
        flip = flips[clip]
        low = jnp.where(flip == 0, from_owner[0], from_owner[1])
        high = jnp.where(flip == 2, from_owner[2], from_owner[3])
        clip_up.append(jnp.where(flip < 2, low, high))
    own_up = jnp.where(live[..., None], jnp.stack(clip_up), jnp.zeros((), jnp.bfloat16))
    own_up = own_up.reshape(own_rows, width)
    to_them = [
        jnp.where(flips[0] == k, 0, jnp.where(flips[1] == k, 1, 2)).astype(jnp.int32)
        for k in range(4)
    ]
    ring, embed_now, limits, *to_them = lax.optimization_barrier(
        (ring, embed_now, limits, *to_them, own_up)
    )[:-1]
    second_operand, out_rows = split_ring(ring.reshape(8 * ROWS, -1))
    qkv_weight = exchange(second_operand, RINGS_SECOND).reshape(width, 3 * HEAD_COLS)

    normed = layer_norm(dot(to_group(encoded), embed_now).astype(jnp.bfloat16))
    upstream = to_group(own_up, qkv_weight, normed)

    qkv = matmul_columns(normed, qkv_weight)
    d_attended = matmul(upstream, out_rows, (1, 1))
    attended, d_qkv = attention(limits, qkv, d_attended)

    term = terms(normed, d_qkv, attended, upstream)
    attended = after(attended, term)
    by_core = attended.reshape(2, 2, own_rows, HEAD_COLS)
    rows_now, rows_across = (
        lax.dynamic_index_in_dim(by_core, which, 1, keepdims=False).reshape(-1, HEAD_COLS)
        for which in (core, 1 - core)
    )
    give_core = send(matmul(rows_across, out_rows), CORE_PARTNER)
    chip = matmul(rows_now, out_rows, add=give_core).reshape(2, own_rows, width)
    give_y = lax.dynamic_index_in_dim(chip, 1 - y_lo, 0, keepdims=False)

    keep = lax.dynamic_index_in_dim(chip, y_lo, 0, keepdims=False)
    projected = keep.astype(jnp.float32) + send(give_y, Y_PARTNER).astype(jnp.float32)
    block = (own_grouped.astype(jnp.float32) + projected).astype(jnp.bfloat16)
    block = block.reshape(clip_count, slab_frames, site_count, width)
    block = jnp.where(live[..., None], block, jnp.zeros((), jnp.bfloat16))
    block = jnp.concatenate([block, jnp.zeros_like(block[:1])])

    def reduced(array, groups, *others):
        parts = after(exchange(array, groups), *others)
        return sum_parts(parts)

    first_sum = reduced(term, RINGS_SECOND, block)
    part = reduced(first_sum.reshape(4, 2 * ROWS, -1), RINGS_FIRST).reshape(2, ROWS, -1)
    part_qkv, part_out = part[..., : 3 * HEAD_COLS], part[..., 3 * HEAD_COLS :]
    even, odd = (
        lax.dynamic_index_in_dim(part_out, which, 0, keepdims=False)
        for which in (place % 2, 1 - place % 2)
    )
    came = in_order(y_lo, send(even, OUT_BACK[0]), send(odd, OUT_BACK[1]))
    mine_out = jnp.concatenate([came[0], came[1]], axis=1)
    mine_qkv = lax.dynamic_index_in_dim(part_qkv, y_lo, 0, keepdims=False)
    other_qkv = lax.dynamic_index_in_dim(part_qkv, 1 - y_lo, 0, keepdims=False)
    across = send(mine_qkv, Y_ACROSS).astype(jnp.float32)
    behind = send(other_qkv, Y_NEXT).astype(jnp.float32)
    before = send(other_qkv, Y_BEFORE).astype(jnp.float32)
    same = mine_qkv.astype(jnp.float32) + across
    cross = behind + before
    sums = jnp.concatenate([same, cross], axis=1)
    across = after(send(mine_out, Y_ACROSS), sums).astype(jnp.float32)
    mine = jnp.concatenate([sums, mine_out.astype(jnp.float32) + across], axis=1)
    theirs = send(mine.astype(jnp.bfloat16), CORE_PARTNER)
    grad_query, grad_key, grad_value, grad_output = final_grads(core, y_lo, mine, theirs)

    arrived = []
    for k in range(4):
        part = lax.dynamic_index_in_dim(block, to_them[k], 0, keepdims=False)
        arrived.append(after(part if k == 0 else send(part, DP_MOVES[k]), sums))
    a0, a1, a2, a3 = arrived
    a0, a1 = jnp.where(core == 0, a0, a1), jnp.where(core == 0, a1, a0)
    a2, a3 = jnp.where(core == 0, a2, a3), jnp.where(core == 0, a3, a2)
    first, second = jnp.stack([a0, a1]), jnp.stack([a2, a3])
    block_out = in_order(y_hi, first, second).reshape(
        1, 4, slab_frames, site_count, width
    )
    return (block_out, grad_query, grad_key, grad_value, grad_output)


def solution(mesh):
    in_specs = (
        P("dp", None, "wide", None, None),
        P(),
        P(),
        P("wide", None),
        P("wide", None),
        P("wide", None),
        P("wide", None),
        P("dp", None, "wide", None, None),
        P(),
        P(),
        P(),
        P(),
    )
    out_specs = (
        P("dp", None, "wide", None, None),
        P("wide", None),
        P("wide", None),
        P("wide", None),
        P("wide", None),
    )
    return jax.shard_map(body, mesh=mesh, in_specs=in_specs, out_specs=out_specs, check_vma=False)
```

```python
import functools
import math

import jax
import jax.numpy as jnp
from jax import lax
from jax.experimental import pallas as pl
from jax.experimental.pallas import tpu as pltpu
from jax.sharding import PartitionSpec as P

HEAD_DIM = 128
EPS = 1e-06
masked_score = -1e30

NO_COST = pl.CostEstimate(flops=0, bytes_accessed=0, transcendentals=0)

ANYWHERE = pl.BlockSpec(memory_space=pl.ANY)

AXES = ("dp", "wide")
N_DEV = 128
N_WIDE = 32
HEAD_COLS = 384
UNIT_ROWS = 128
UNITS = 2
ROWS = 48


def place_of(index):
    dp, wide = divmod(index, N_WIDE)
    y_hi, core = divmod(dp, 2)
    z, rest = divmod(wide, 8)
    x, y_lo = divmod(rest, 2)
    return core, x, y_hi * 2 + y_lo, z


def index_of(core, x, y, z):
    y_hi, y_lo = divmod(y % 4, 2)
    return (y_hi * 2 + core % 2) * N_WIDE + (z % 4) * 8 + (x % 4) * 2 + y_lo


def pairs_by(move):
    return [(i, index_of(*move(*place_of(i)))) for i in range(N_DEV)]


Y_PARTNER = pairs_by(lambda core, x, y, z: (core, x, y ^ 1, z))
CORE_PARTNER = pairs_by(lambda core, x, y, z: (core ^ 1, x, y, z))
Y_NEXT = pairs_by(lambda core, x, y, z: (core, x, y + 1, z))
Y_BEFORE = pairs_by(lambda core, x, y, z: (core, x, y - 1, z))
Y_ACROSS = pairs_by(lambda core, x, y, z: (core, x, y + 2, z))
DP_MOVES = [[(i, i ^ (k * N_WIDE)) for i in range(N_DEV)] for k in range(4)]
HALO = [(i, i + 1) for i in range(N_DEV) if (i + 1) % N_WIDE]


def output_source(core, x, y, z, flip):
    y_hi, y_lo = divmod(y, 2)
    place, across = (z, x) if core else (x, z)
    return index_of(across // 2, place, y_hi * 2 + ((across % 2) ^ flip), 2 * y_lo + core)


RING_FLIPS = [
    pairs_by(lambda core, x, y, z, k=k: (core, x, y, z ^ k) if core else (core, x ^ k, y, z))
    for k in range(4)
]


OUT_PAIRS = [[(output_source(*place_of(i), flip), i) for i in range(N_DEV)] for flip in (0, 1)]
def spot(index):
    core, x, _, z = place_of(index)
    return z if core else x


def output_target(core, x, y, z, block):
    y_hi, y_lo = divmod(y, 2)
    place, column = (x, z) if core else (z, x)
    return index_of(column // 2, place, y_hi * 2 + block, 2 * y_lo + core)


OUT_BACK = [
    [(i, output_target(*place_of(i), block=(spot(i) % 2) ^ flip)) for i in range(N_DEV)]
    for flip in (0, 1)
]


def rings(axis_of_core):
    groups = []
    for core in range(2):
        for a in range(4):
            for y in range(4):
                if axis_of_core[core] == "z":
                    groups.append([index_of(core, a, y, z) for z in range(4)])
                else:
                    groups.append([index_of(core, x, y, a) for x in range(4)])
    return groups


RINGS_FIRST = rings("xz")
RINGS_SECOND = rings("zx")


def send(array, pairs):
    return lax.ppermute(array, AXES, pairs)


def exchange(array, groups):
    return lax.all_to_all(array, AXES, 0, 0, tiled=True, axis_index_groups=groups)


def spread(array):
    return jnp.broadcast_to(array[None], (4,) + array.shape)


def in_order(bit, mine, other, axis=0):
    return jnp.stack([jnp.where(bit == 0, mine, other), jnp.where(bit == 0, other, mine)], axis)


def after(value, *others):
    return lax.optimization_barrier((value,) + others)[0]


def embed_kernel(rows_ref, weight_ref, out_ref):
    values = dot(rows_ref[...], weight_ref[...]).astype(jnp.bfloat16)
    out_ref[...] = layer_norm(values)


def embed_and_norm(rows, weight):
    tile = 256
    return pl.pallas_call(
        embed_kernel,
        grid=(rows.shape[0] // tile,),
        in_specs=[
            pl.BlockSpec((tile, rows.shape[1]), lambda i: (i, 0)),
            pl.BlockSpec(weight.shape, lambda i: (0, 0)),
        ],
        out_specs=pl.BlockSpec((tile, weight.shape[1]), lambda i: (i, 0)),
        out_shape=jax.ShapeDtypeStruct((rows.shape[0], weight.shape[1]), jnp.bfloat16),
        compiler_params=pltpu.CompilerParams(vmem_limit_bytes=32 * 1024 * 1024),
        cost_estimate=NO_COST,
    )(rows, weight)


def layer_norm(values):
    floats = values.astype(jnp.float32)
    center = floats - jnp.mean(floats, axis=-1, keepdims=True)
    spread = jnp.mean(center * center, axis=-1, keepdims=True)
    return (center * lax.rsqrt(spread + EPS)).astype(jnp.bfloat16)


def dot(a, b, dims=((1,), (0,))):
    return lax.dot_general(a, b, (dims, ((), ())), preferred_element_type=jnp.float32)


def product_kernel(dims, added, a_ref, b_ref, *rest):
    product = dot(a_ref[...], b_ref[...], dims)
    if added:
        product = product + rest[0][...].astype(jnp.float32)
    rest[-1][...] = product.astype(jnp.bfloat16)


def matmul(a, b, dims=(1, 0), tile=256, add=None, others=()):
    rows, depth = a.shape[1 - dims[0]], a.shape[dims[0]]
    columns = b.shape[1 - dims[1]]
    if dims[0]:
        a_spec = pl.BlockSpec((tile, depth), lambda i: (i, 0))
    else:
        a_spec = pl.BlockSpec((depth, tile), lambda i: (0, i))
    out_spec = pl.BlockSpec((tile, columns), lambda i: (i, 0))
    return pl.pallas_call(
        functools.partial(product_kernel, ((dims[0],), (dims[1],)), add is not None),
        grid=(rows // tile,),
        in_specs=[a_spec, pl.BlockSpec(b.shape, lambda i: (0, 0))]
        + ([out_spec] if add is not None else [])
        + [ANYWHERE] * len(others),
        out_specs=out_spec,
        out_shape=jax.ShapeDtypeStruct((rows, columns), jnp.bfloat16),
        compiler_params=pltpu.CompilerParams(vmem_limit_bytes=40 * 1024 * 1024),
        cost_estimate=NO_COST,
    )(*((a, b) if add is None else (a, b, add)), *others)


def matmul_columns(a, b):
    rows, depth = a.shape
    return pl.pallas_call(
        functools.partial(product_kernel, ((1,), (0,)), False),
        grid=(3,),
        in_specs=[
            pl.BlockSpec((rows, depth), lambda i: (0, 0)),
            pl.BlockSpec((depth, HEAD_COLS), lambda i: (0, i)),
        ],
        out_specs=pl.BlockSpec((rows, HEAD_COLS), lambda i: (0, i)),
        out_shape=jax.ShapeDtypeStruct((rows, b.shape[1]), jnp.bfloat16),
        compiler_params=pltpu.CompilerParams(vmem_limit_bytes=40 * 1024 * 1024),
        cost_estimate=NO_COST,
    )(a, b)


def split_kernel(ring_ref, spread_ref, out_ref):
    spread_ref[0] = ring_ref[:, : 3 * HEAD_COLS]

    @pl.when(pl.program_id(0) == 0)
    def _():
        out_ref[...] = ring_ref[:, 3 * HEAD_COLS :]


def split_ring(ring):
    rows, width = ring.shape[0], ring.shape[1] - 3 * HEAD_COLS
    return pl.pallas_call(
        split_kernel,
        grid=(4,),
        in_specs=[pl.BlockSpec(ring.shape, lambda i: (0, 0))],
        out_specs=[
            pl.BlockSpec((1, rows, 3 * HEAD_COLS), lambda i: (i, 0, 0)),
            pl.BlockSpec((rows, width), lambda i: (0, 0)),
        ],
        out_shape=[
            pltpu.HBM((4, rows, 3 * HEAD_COLS), jnp.bfloat16),
            jax.ShapeDtypeStruct((rows, width), jnp.bfloat16),
        ],
        compiler_params=pltpu.CompilerParams(vmem_limit_bytes=32 * 1024 * 1024),
        cost_estimate=NO_COST,
    )(ring)


def term_kernel(normed_ref, d_qkv_ref, att_ref, up_ref, out_ref, total_ref):
    out_ref[0, :, : 3 * HEAD_COLS] = dot(
        normed_ref[...], d_qkv_ref[...], ((0,), (0,))
    ).astype(jnp.bfloat16)

    @pl.when(pl.program_id(0) == 0)
    def _():
        total_ref[...] = dot(att_ref[...], up_ref[...], ((0,), (0,))).astype(jnp.bfloat16)

    at = pl.multiple_of(pl.program_id(0) * 2 * ROWS, 2 * ROWS)
    for block in range(4):
        out_ref[0, block * 2 * ROWS : (block + 1) * 2 * ROWS, 3 * HEAD_COLS :] = total_ref[
            pl.ds(at, 2 * ROWS), block * HEAD_COLS : (block + 1) * HEAD_COLS
        ]


def terms(normed, d_qkv, attended, upstream):
    depth, width = normed.shape
    rows = width // 4
    whole = lambda array: pl.BlockSpec(array.shape, lambda i: (0, 0))
    return pl.pallas_call(
        term_kernel,
        grid=(4,),
        in_specs=[
            pl.BlockSpec((depth, rows), lambda i: (0, i)),
            whole(d_qkv),
            whole(attended),
            whole(upstream),
        ],
        out_specs=pl.BlockSpec((1, rows, 4 * HEAD_COLS), lambda i: (i, 0, 0)),
        out_shape=pltpu.HBM((4, rows, 4 * HEAD_COLS), jnp.bfloat16),
        scratch_shapes=[pltpu.VMEM((HEAD_COLS, width), jnp.bfloat16)],
        compiler_params=pltpu.CompilerParams(vmem_limit_bytes=40 * 1024 * 1024),
        cost_estimate=NO_COST,
    )(normed, d_qkv, attended, upstream)


def sum_kernel(parts_ref, *rest):
    out_ref = rest[-1]
    total = parts_ref[0].astype(jnp.float32)
    for i in range(1, 4):
        total = total + parts_ref[i].astype(jnp.float32)
    out_ref[...] = total.astype(jnp.bfloat16)


def sum_parts(parts, *others):
    rows, width = parts.shape[1:]
    tile = 2 * ROWS if rows > 2 * ROWS else ROWS
    return pl.pallas_call(
        sum_kernel,
        grid=(rows // tile,),
        in_specs=[pl.BlockSpec((4, tile, width), lambda i: (0, i, 0))] + [ANYWHERE] * len(others),
        out_specs=pl.BlockSpec((tile, width), lambda i: (i, 0)),
        out_shape=jax.ShapeDtypeStruct((rows, width), jnp.bfloat16),
        compiler_params=pltpu.CompilerParams(vmem_limit_bytes=32 * 1024 * 1024),
        cost_estimate=NO_COST,
    )(parts, *others)


def final_kernel(place_ref, mine_ref, theirs_ref, query_ref, key_ref, value_ref, output_ref):
    core, y_lo = place_ref[0], place_ref[1]
    wide = 3 * HEAD_COLS
    for kind, out in enumerate((query_ref, key_ref, value_ref)):
        for step in range(2):
            at = step * wide + kind * HEAD_COLS
            mine = mine_ref[:, at : at + HEAD_COLS]
            theirs = theirs_ref[:, at : at + HEAD_COLS].astype(jnp.float32)
            low = jnp.where(core == 0, mine, theirs)
            high = jnp.where(core == 0, theirs, mine)
            for side in range(2):

                @pl.when((y_lo ^ step) == side)
                def _():
                    begin = 2 * side * HEAD_COLS
                    out[:, begin : begin + HEAD_COLS] = low
                    out[:, begin + HEAD_COLS : begin + 2 * HEAD_COLS] = high

    mine = mine_ref[:, 2 * wide :]
    theirs = theirs_ref[:, 2 * wide :].astype(jnp.float32)
    output_ref[:, : 2 * HEAD_COLS] = jnp.where(core == 0, mine, theirs)
    output_ref[:, 2 * HEAD_COLS :] = jnp.where(core == 0, theirs, mine)


def final_grads(core, y_lo, mine, theirs):
    rows, width = mine.shape[0], 4 * HEAD_COLS
    whole = pl.BlockSpec(memory_space=pltpu.VMEM)
    return pl.pallas_call(
        final_kernel,
        in_specs=[pl.BlockSpec(memory_space=pltpu.SMEM), whole, whole],
        out_specs=[whole] * 4,
        out_shape=[jax.ShapeDtypeStruct((rows, width), jnp.float32)] * 4,
        cost_estimate=NO_COST,
    )(jnp.stack([core, y_lo]).astype(jnp.int32), mine, theirs)


def attention_kernel(limit_ref, qkv_ref, d_att_ref, att_ref, grads_ref):
    rows = UNIT_ROWS
    sites = rows // 2
    scale = 1.0 / math.sqrt(HEAD_DIM)
    row = lax.broadcasted_iota(jnp.int32, (rows, rows), 0)
    col = lax.broadcasted_iota(jnp.int32, (rows, rows), 1)
    upper = col >= sites
    site = jnp.where(upper, col - sites, col)
    block = upper == (row >= sites)
    masks = [
        block & (site < limit_ref[pl.program_id(0) * UNITS + unit]) for unit in range(UNITS)
    ]
    units = [(unit, head) for unit in range(UNITS) for head in range(HEAD_COLS // HEAD_DIM)]

    def part(ref, unit, head, kind):
        return ref[
            unit * rows : (unit + 1) * rows,
            kind * HEAD_COLS + head * HEAD_DIM : kind * HEAD_COLS + (head + 1) * HEAD_DIM,
        ]

    def put(ref, unit, head, kind, value):
        ref[
            unit * rows : (unit + 1) * rows,
            kind * HEAD_COLS + head * HEAD_DIM : kind * HEAD_COLS + (head + 1) * HEAD_DIM,
        ] = value.astype(jnp.bfloat16)

    scores = [
        dot(part(qkv_ref, u, h, 0), part(qkv_ref, u, h, 1), ((1,), (1,))) for u, h in units
    ]
    d_probs = [
        dot(part(d_att_ref, u, h, 0), part(qkv_ref, u, h, 2), ((1,), (1,))) for u, h in units
    ]
    low = []
    d_scores = []
    for (u, h), score, d_prob in zip(units, scores, d_probs):
        score = jnp.where(masks[u], score * scale, masked_score)
        weights = jnp.exp(score - jnp.max(score, axis=-1, keepdims=True))
        probs = weights * (1.0 / jnp.sum(weights, axis=-1, keepdims=True))
        inner = jnp.sum(probs * d_prob, axis=-1, keepdims=True)
        low.append(probs.astype(jnp.bfloat16))
        d_scores.append((probs * (d_prob - inner) * scale).astype(jnp.bfloat16))
    for (u, h), prob, d_score in zip(units, low, d_scores):
        put(att_ref, u, h, 0, dot(prob, part(qkv_ref, u, h, 2)))
        put(grads_ref, u, h, 0, dot(d_score, part(qkv_ref, u, h, 1)))
        put(grads_ref, u, h, 1, dot(d_score, part(qkv_ref, u, h, 0), ((0,), (0,))))
        put(grads_ref, u, h, 2, dot(prob, part(d_att_ref, u, h, 0), ((0,), (0,))))


def attention(limits, qkv, d_att):
    rows = UNITS * UNIT_ROWS
    count = qkv.shape[0] // rows
    spec = lambda width: pl.BlockSpec((rows, width), lambda i, limits: (i, 0))
    return pl.pallas_call(
        attention_kernel,
        grid_spec=pltpu.PrefetchScalarGridSpec(
            num_scalar_prefetch=1,
            grid=(count,),
            in_specs=[spec(3 * HEAD_COLS), spec(HEAD_COLS)],
            out_specs=[spec(HEAD_COLS), spec(3 * HEAD_COLS)],
        ),
        out_shape=[
            jax.ShapeDtypeStruct((qkv.shape[0], HEAD_COLS), jnp.bfloat16),
            jax.ShapeDtypeStruct((qkv.shape[0], 3 * HEAD_COLS), jnp.bfloat16),
        ],
        compiler_params=pltpu.CompilerParams(vmem_limit_bytes=32 * 1024 * 1024),
        cost_estimate=NO_COST,
    )(limits, qkv, d_att)


def body(
    frames,
    conv_weight,
    embed_weight,
    query_weight,
    key_weight,
    value_weight,
    output_weight,
    out_grad,
    bucket_owner,
    clip_bucket,
    clip_frames,
    clip_grid,
):
    my_dp = lax.axis_index("dp")
    my_slab = lax.axis_index("wide")
    core, y_hi = my_dp % 2, my_dp // 2
    y_lo = my_slab % 2
    heads_now = 2 * y_lo + core
    heads_across = 2 * (1 - y_lo) + core
    frame_slab = frames[0]
    clip_count, slab_frames, site_count, channels = frame_slab.shape
    width = embed_weight.shape[1]
    own_rows = clip_count * slab_frames * site_count

    def head_columns(which):
        return jnp.concatenate(
            [
                lax.dynamic_slice(w, (0, which * HEAD_COLS), (ROWS, HEAD_COLS))
                for w in (query_weight, key_weight, value_weight)
            ],
            axis=1,
        )

    x_place, z_place = (my_slab // 2) % 4, my_slab // 8
    place = jnp.where(core == 0, x_place, z_place)
    across_place = jnp.where(core == 0, z_place, x_place)
    parity = across_place % 2

    outgoing = head_columns(heads_across)
    grads, outgoing = lax.optimization_barrier((out_grad[0], outgoing))
    pair = in_order(y_lo, head_columns(heads_now), send(outgoing, Y_PARTNER))
    pair, frame_slab = lax.optimization_barrier((pair, frame_slab))
    out_pair = in_order(
        parity, send(output_weight, OUT_PAIRS[0]), send(output_weight, OUT_PAIRS[1])
    )
    first_operand = spread(jnp.concatenate([pair, out_pair], axis=2))
    embed_weight = after(embed_weight, first_operand)
    earlier = send(frame_slab, HALO)
    bucket_owner, clip_bucket, clip_frames, clip_grid = lax.optimization_barrier(
        (bucket_owner, clip_bucket, clip_frames, clip_grid, earlier)
    )[:-1]
    ring = exchange(first_operand, RINGS_FIRST)
    owners = bucket_owner[clip_bucket]
    tokens = clip_grid[..., 0] * clip_grid[..., 1]
    my_owners = owners[my_dp]
    frame_pos = my_slab * slab_frames + jnp.arange(slab_frames, dtype=jnp.int32)
    site_pos = jnp.arange(site_count, dtype=jnp.int32)
    live = (frame_pos[None, :, None] < clip_frames[my_dp][:, None, None]) & (
        site_pos[None, None, :] < tokens[my_dp][:, None, None]
    )
    group_tokens = lax.dynamic_slice(tokens, (2 * y_hi, 0), (2, clip_count)).reshape(-1)
    limits = jnp.concatenate([group_tokens, group_tokens])

    def to_group(own, *others):
        both = in_order(y_lo, own, after(send(own, Y_PARTNER), *others))
        return in_order(core, both, send(both, CORE_PARTNER), axis=1).reshape(-1, own.shape[-1])

    joined = jnp.concatenate([earlier, frame_slab], axis=1)
    active = jax.nn.silu(joined.astype(jnp.float32)).astype(jnp.bfloat16)
    summed = frame_slab.astype(jnp.float32).reshape(-1, channels)
    for offset in range(3):
        moved = active[:, slab_frames - offset : 2 * slab_frames - offset].reshape(-1, channels)
        summed = summed + dot(moved, conv_weight[offset])
    encoded = summed.astype(jnp.bfloat16)
    own_grouped = dot(encoded, embed_weight).astype(jnp.bfloat16)
    swapped = embed_weight.reshape(channels, 4, 4, -1).swapaxes(1, 2).reshape(channels, width)
    embed_now = jnp.where(core == 0, embed_weight, swapped)

    flips = [my_owners[clip] ^ my_dp for clip in range(clip_count)]
    from_owner = []
    for k in range(4):
        part = lax.dynamic_index_in_dim(grads, my_dp ^ k, 0, keepdims=False)
        part = after(part, first_operand) if k == 1 else part
        from_owner.append(part if k == 0 else send(part, DP_MOVES[k]))
    to_them = [
        jnp.where(flips[0] == k, 0, jnp.where(flips[1] == k, 1, 2)).astype(jnp.int32)
        for k in range(4)
    ]
    ring, embed_now, limits, *to_them = lax.optimization_barrier(
        (ring, embed_now, limits, *to_them)
    )
    from_owner = [after(part, ring) for part in from_owner]
    clip_up = []
    for clip in range(clip_count):
        flip = flips[clip]
        low = jnp.where(flip == 0, from_owner[0], from_owner[1])
        high = jnp.where(flip == 2, from_owner[2], from_owner[3])
        clip_up.append(jnp.where(flip < 2, low, high))
    own_up = jnp.where(live[..., None], jnp.stack(clip_up), jnp.zeros((), jnp.bfloat16))
    own_up = own_up.reshape(own_rows, width)
    second_operand, out_rows = split_ring(ring.reshape(8 * ROWS, -1))
    qkv_weight = exchange(second_operand, RINGS_SECOND).reshape(width, 3 * HEAD_COLS)

    normed = embed_and_norm(to_group(encoded, ring), embed_now)
    upstream = to_group(own_up, qkv_weight, normed)

    qkv = matmul_columns(normed, qkv_weight)
    d_attended = matmul(upstream, out_rows, (1, 1))
    attended, d_qkv = attention(limits, qkv, d_attended)

    term = terms(normed, d_qkv, attended, upstream)
    attended, term = lax.optimization_barrier((attended, term))
    by_core = attended.reshape(2, 2, own_rows, HEAD_COLS)
    rows_now, rows_across = (
        lax.dynamic_index_in_dim(by_core, which, 1, keepdims=False).reshape(-1, HEAD_COLS)
        for which in (core, 1 - core)
    )
    give_core = send(matmul(rows_across, out_rows), CORE_PARTNER)
    chip = matmul(rows_now, out_rows, add=give_core).reshape(2, own_rows, width)
    give_y = lax.dynamic_index_in_dim(chip, 1 - y_lo, 0, keepdims=False)

    keep = lax.dynamic_index_in_dim(chip, y_lo, 0, keepdims=False)
    projected = keep.astype(jnp.float32) + send(give_y, Y_PARTNER).astype(jnp.float32)
    block = (own_grouped.astype(jnp.float32) + projected).astype(jnp.bfloat16)
    block = block.reshape(clip_count, slab_frames, site_count, width)
    block = jnp.where(live[..., None], block, jnp.zeros((), jnp.bfloat16))
    block = jnp.concatenate([block, jnp.zeros_like(block[:1])])

    arrived, sent = [], []
    for k in range(4):
        part = lax.dynamic_index_in_dim(block, to_them[k], 0, keepdims=False)
        sent.append(part)
        arrived.append(part if k == 0 else send(part, DP_MOVES[k]))

    def reduced(array, groups, *others):
        return sum_parts(exchange(array, groups), *others)

    first_sum = reduced(term, RINGS_SECOND, *sent[1:])
    part = reduced(first_sum.reshape(4, 2 * ROWS, -1), RINGS_FIRST)
    part = part.reshape(2, ROWS, -1)
    part_qkv, part_out = part[..., : 3 * HEAD_COLS], part[..., 3 * HEAD_COLS :]
    even, odd = (
        lax.dynamic_index_in_dim(part_out, which, 0, keepdims=False)
        for which in (place % 2, 1 - place % 2)
    )
    came = in_order(y_lo, send(even, OUT_BACK[0]), send(odd, OUT_BACK[1]))
    mine_out = jnp.concatenate([came[0], came[1]], axis=1)
    mine_qkv = lax.dynamic_index_in_dim(part_qkv, y_lo, 0, keepdims=False)
    other_qkv = lax.dynamic_index_in_dim(part_qkv, 1 - y_lo, 0, keepdims=False)
    across = send(mine_qkv, Y_ACROSS).astype(jnp.float32)
    behind = send(other_qkv, Y_NEXT).astype(jnp.float32)
    before = send(other_qkv, Y_BEFORE).astype(jnp.float32)
    same = mine_qkv.astype(jnp.float32) + across
    cross = behind + before
    sums = jnp.concatenate([same, cross], axis=1)
    across = after(send(mine_out, Y_ACROSS), sums).astype(jnp.float32)
    mine = jnp.concatenate([sums, mine_out.astype(jnp.float32) + across], axis=1)
    theirs = send(mine.astype(jnp.bfloat16), CORE_PARTNER)
    grad_query, grad_key, grad_value, grad_output = final_grads(core, y_lo, mine, theirs)

    a0, a1, a2, a3 = (after(part, sums) for part in arrived)
    a0, a1 = jnp.where(core == 0, a0, a1), jnp.where(core == 0, a1, a0)
    a2, a3 = jnp.where(core == 0, a2, a3), jnp.where(core == 0, a3, a2)
    first, second = jnp.stack([a0, a1]), jnp.stack([a2, a3])
    block_out = in_order(y_hi, first, second).reshape(
        1, 4, slab_frames, site_count, width
    )
    return (block_out, grad_query, grad_key, grad_value, grad_output)


def solution(mesh):
    in_specs = (
        P("dp", None, "wide", None, None),
        P(),
        P(),
        P("wide", None),
        P("wide", None),
        P("wide", None),
        P("wide", None),
        P("dp", None, "wide", None, None),
        P(),
        P(),
        P(),
        P(),
    )
    out_specs = (
        P("dp", None, "wide", None, None),
        P("wide", None),
        P("wide", None),
        P("wide", None),
        P("wide", None),
    )
    return jax.shard_map(body, mesh=mesh, in_specs=in_specs, out_specs=out_specs, check_vma=False)
```

```python
import functools
import math

import jax
import jax.numpy as jnp
from jax import lax
from jax.experimental import pallas as pl
from jax.experimental.pallas import tpu as pltpu
from jax.sharding import PartitionSpec as P

HEAD_DIM = 128
EPS = 1e-06
masked_score = -1e30

NO_COST = pl.CostEstimate(flops=0, bytes_accessed=0, transcendentals=0)

ANYWHERE = pl.BlockSpec(memory_space=pl.ANY)

AXES = ("dp", "wide")
N_DEV = 128
N_WIDE = 32
HEAD_COLS = 384
UNIT_ROWS = 128
UNITS = 2
ROWS = 48


def place_of(index):
    dp, wide = divmod(index, N_WIDE)
    y_hi, core = divmod(dp, 2)
    z, rest = divmod(wide, 8)
    x, y_lo = divmod(rest, 2)
    return core, x, y_hi * 2 + y_lo, z


def index_of(core, x, y, z):
    y_hi, y_lo = divmod(y % 4, 2)
    return (y_hi * 2 + core % 2) * N_WIDE + (z % 4) * 8 + (x % 4) * 2 + y_lo


def pairs_by(move):
    return [(i, index_of(*move(*place_of(i)))) for i in range(N_DEV)]


Y_PARTNER = pairs_by(lambda core, x, y, z: (core, x, y ^ 1, z))
CORE_PARTNER = pairs_by(lambda core, x, y, z: (core ^ 1, x, y, z))
Y_NEXT = pairs_by(lambda core, x, y, z: (core, x, y + 1, z))
Y_BEFORE = pairs_by(lambda core, x, y, z: (core, x, y - 1, z))
Y_ACROSS = pairs_by(lambda core, x, y, z: (core, x, y + 2, z))
DP_MOVES = [[(i, i ^ (k * N_WIDE)) for i in range(N_DEV)] for k in range(4)]
HALO = [(i, i + 1) for i in range(N_DEV) if (i + 1) % N_WIDE]


def output_source(core, x, y, z, flip):
    y_hi, y_lo = divmod(y, 2)
    place, across = (z, x) if core else (x, z)
    return index_of(across // 2, place, y_hi * 2 + ((across % 2) ^ flip), 2 * y_lo + core)


RING_FLIPS = [
    pairs_by(lambda core, x, y, z, k=k: (core, x, y, z ^ k) if core else (core, x ^ k, y, z))
    for k in range(4)
]


OUT_PAIRS = [[(output_source(*place_of(i), flip), i) for i in range(N_DEV)] for flip in (0, 1)]
def spot(index):
    core, x, _, z = place_of(index)
    return z if core else x


def output_target(core, x, y, z, block):
    y_hi, y_lo = divmod(y, 2)
    place, column = (x, z) if core else (z, x)
    return index_of(column // 2, place, y_hi * 2 + block, 2 * y_lo + core)


OUT_BACK = [
    [(i, output_target(*place_of(i), block=(spot(i) % 2) ^ flip)) for i in range(N_DEV)]
    for flip in (0, 1)
]


def rings(axis_of_core):
    groups = []
    for core in range(2):
        for a in range(4):
            for y in range(4):
                if axis_of_core[core] == "z":
                    groups.append([index_of(core, a, y, z) for z in range(4)])
                else:
                    groups.append([index_of(core, x, y, a) for x in range(4)])
    return groups


RINGS_FIRST = rings("xz")
RINGS_SECOND = rings("zx")


def send(array, pairs):
    return lax.ppermute(array, AXES, pairs)


def exchange(array, groups):
    return lax.all_to_all(array, AXES, 0, 0, tiled=True, axis_index_groups=groups)


def spread(array):
    return jnp.broadcast_to(array[None], (4,) + array.shape)


def in_order(bit, mine, other, axis=0):
    return jnp.stack([jnp.where(bit == 0, mine, other), jnp.where(bit == 0, other, mine)], axis)


def after(value, *others):
    return lax.optimization_barrier((value,) + others)[0]


def embed_kernel(rows_ref, weight_ref, out_ref):
    values = dot(rows_ref[...], weight_ref[...]).astype(jnp.bfloat16)
    out_ref[...] = layer_norm(values)


def embed_and_norm(rows, weight):
    tile = 256
    return pl.pallas_call(
        embed_kernel,
        grid=(rows.shape[0] // tile,),
        in_specs=[
            pl.BlockSpec((tile, rows.shape[1]), lambda i: (i, 0)),
            pl.BlockSpec(weight.shape, lambda i: (0, 0)),
        ],
        out_specs=pl.BlockSpec((tile, weight.shape[1]), lambda i: (i, 0)),
        out_shape=jax.ShapeDtypeStruct((rows.shape[0], weight.shape[1]), jnp.bfloat16),
        compiler_params=pltpu.CompilerParams(vmem_limit_bytes=32 * 1024 * 1024),
        cost_estimate=NO_COST,
    )(rows, weight)


def layer_norm(values):
    floats = values.astype(jnp.float32)
    center = floats - jnp.mean(floats, axis=-1, keepdims=True)
    spread = jnp.mean(center * center, axis=-1, keepdims=True)
    return (center * lax.rsqrt(spread + EPS)).astype(jnp.bfloat16)


def dot(a, b, dims=((1,), (0,))):
    return lax.dot_general(a, b, (dims, ((), ())), preferred_element_type=jnp.float32)


def product_kernel(dims, added, a_ref, b_ref, *rest):
    product = dot(a_ref[...], b_ref[...], dims)
    if added:
        product = product + rest[0][...].astype(jnp.float32)
    rest[-1][...] = product.astype(jnp.bfloat16)


def matmul(a, b, dims=(1, 0), tile=256, add=None, others=()):
    rows, depth = a.shape[1 - dims[0]], a.shape[dims[0]]
    columns = b.shape[1 - dims[1]]
    if dims[0]:
        a_spec = pl.BlockSpec((tile, depth), lambda i: (i, 0))
    else:
        a_spec = pl.BlockSpec((depth, tile), lambda i: (0, i))
    out_spec = pl.BlockSpec((tile, columns), lambda i: (i, 0))
    return pl.pallas_call(
        functools.partial(product_kernel, ((dims[0],), (dims[1],)), add is not None),
        grid=(rows // tile,),
        in_specs=[a_spec, pl.BlockSpec(b.shape, lambda i: (0, 0))]
        + ([out_spec] if add is not None else [])
        + [ANYWHERE] * len(others),
        out_specs=out_spec,
        out_shape=jax.ShapeDtypeStruct((rows, columns), jnp.bfloat16),
        compiler_params=pltpu.CompilerParams(vmem_limit_bytes=40 * 1024 * 1024),
        cost_estimate=NO_COST,
    )(*((a, b) if add is None else (a, b, add)), *others)


def matmul_columns(a, b):
    rows, depth = a.shape
    return pl.pallas_call(
        functools.partial(product_kernel, ((1,), (0,)), False),
        grid=(3,),
        in_specs=[
            pl.BlockSpec((rows, depth), lambda i: (0, 0)),
            pl.BlockSpec((depth, HEAD_COLS), lambda i: (0, i)),
        ],
        out_specs=pl.BlockSpec((rows, HEAD_COLS), lambda i: (0, i)),
        out_shape=jax.ShapeDtypeStruct((rows, b.shape[1]), jnp.bfloat16),
        compiler_params=pltpu.CompilerParams(vmem_limit_bytes=40 * 1024 * 1024),
        cost_estimate=NO_COST,
    )(a, b)


def split_kernel(ring_ref, spread_ref, out_ref):
    spread_ref[0] = ring_ref[:, : 3 * HEAD_COLS]

    @pl.when(pl.program_id(0) == 0)
    def _():
        out_ref[...] = ring_ref[:, 3 * HEAD_COLS :]


def split_ring(ring):
    rows, width = ring.shape[0], ring.shape[1] - 3 * HEAD_COLS
    return pl.pallas_call(
        split_kernel,
        grid=(4,),
        in_specs=[pl.BlockSpec(ring.shape, lambda i: (0, 0))],
        out_specs=[
            pl.BlockSpec((1, rows, 3 * HEAD_COLS), lambda i: (i, 0, 0)),
            pl.BlockSpec((rows, width), lambda i: (0, 0)),
        ],
        out_shape=[
            pltpu.HBM((4, rows, 3 * HEAD_COLS), jnp.bfloat16),
            jax.ShapeDtypeStruct((rows, width), jnp.bfloat16),
        ],
        compiler_params=pltpu.CompilerParams(vmem_limit_bytes=32 * 1024 * 1024),
        cost_estimate=NO_COST,
    )(ring)


def term_kernel(normed_ref, d_qkv_ref, att_ref, up_ref, out_ref, total_ref):
    out_ref[0, :, : 3 * HEAD_COLS] = dot(
        normed_ref[...], d_qkv_ref[...], ((0,), (0,))
    ).astype(jnp.bfloat16)

    @pl.when(pl.program_id(0) == 0)
    def _():
        total_ref[...] = dot(att_ref[...], up_ref[...], ((0,), (0,))).astype(jnp.bfloat16)

    at = pl.multiple_of(pl.program_id(0) * 2 * ROWS, 2 * ROWS)
    for block in range(4):
        out_ref[0, block * 2 * ROWS : (block + 1) * 2 * ROWS, 3 * HEAD_COLS :] = total_ref[
            pl.ds(at, 2 * ROWS), block * HEAD_COLS : (block + 1) * HEAD_COLS
        ]


def terms(normed, d_qkv, attended, upstream):
    depth, width = normed.shape
    rows = width // 4
    whole = lambda array: pl.BlockSpec(array.shape, lambda i: (0, 0))
    return pl.pallas_call(
        term_kernel,
        grid=(4,),
        in_specs=[
            pl.BlockSpec((depth, rows), lambda i: (0, i)),
            whole(d_qkv),
            whole(attended),
            whole(upstream),
        ],
        out_specs=pl.BlockSpec((1, rows, 4 * HEAD_COLS), lambda i: (i, 0, 0)),
        out_shape=pltpu.HBM((4, rows, 4 * HEAD_COLS), jnp.bfloat16),
        scratch_shapes=[pltpu.VMEM((HEAD_COLS, width), jnp.bfloat16)],
        compiler_params=pltpu.CompilerParams(vmem_limit_bytes=40 * 1024 * 1024),
        cost_estimate=NO_COST,
    )(normed, d_qkv, attended, upstream)


def sum_kernel(parts_ref, *rest):
    out_ref = rest[-1]
    total = parts_ref[0].astype(jnp.float32)
    for i in range(1, 4):
        total = total + parts_ref[i].astype(jnp.float32)
    out_ref[...] = total.astype(jnp.bfloat16)


def sum_parts(parts, *others):
    rows, width = parts.shape[1:]
    tile = 2 * ROWS if rows > 2 * ROWS else ROWS
    return pl.pallas_call(
        sum_kernel,
        grid=(rows // tile,),
        in_specs=[pl.BlockSpec((4, tile, width), lambda i: (0, i, 0))] + [ANYWHERE] * len(others),
        out_specs=pl.BlockSpec((tile, width), lambda i: (i, 0)),
        out_shape=jax.ShapeDtypeStruct((rows, width), jnp.bfloat16),
        compiler_params=pltpu.CompilerParams(vmem_limit_bytes=32 * 1024 * 1024),
        cost_estimate=NO_COST,
    )(parts, *others)


def final_kernel(place_ref, mine_ref, theirs_ref, query_ref, key_ref, value_ref, output_ref):
    core, y_lo = place_ref[0], place_ref[1]
    wide = 3 * HEAD_COLS
    for kind, out in enumerate((query_ref, key_ref, value_ref)):
        for step in range(2):
            at = step * wide + kind * HEAD_COLS
            mine = mine_ref[:, at : at + HEAD_COLS].astype(jnp.float32)
            theirs = theirs_ref[:, at : at + HEAD_COLS].astype(jnp.float32)
            low = jnp.where(core == 0, mine, theirs)
            high = jnp.where(core == 0, theirs, mine)
            for side in range(2):

                @pl.when((y_lo ^ step) == side)
                def _():
                    begin = 2 * side * HEAD_COLS
                    out[:, begin : begin + HEAD_COLS] = low
                    out[:, begin + HEAD_COLS : begin + 2 * HEAD_COLS] = high

    mine = mine_ref[:, 2 * wide :].astype(jnp.float32)
    theirs = theirs_ref[:, 2 * wide :].astype(jnp.float32)
    output_ref[:, : 2 * HEAD_COLS] = jnp.where(core == 0, mine, theirs)
    output_ref[:, 2 * HEAD_COLS :] = jnp.where(core == 0, theirs, mine)


def final_grads(core, y_lo, mine, theirs):
    rows, width = mine.shape[0], 4 * HEAD_COLS
    whole = pl.BlockSpec(memory_space=pltpu.VMEM)
    return pl.pallas_call(
        final_kernel,
        in_specs=[pl.BlockSpec(memory_space=pltpu.SMEM), whole, whole],
        out_specs=[whole] * 4,
        out_shape=[jax.ShapeDtypeStruct((rows, width), jnp.float32)] * 4,
        cost_estimate=NO_COST,
    )(jnp.stack([core, y_lo]).astype(jnp.int32), mine, theirs)


def attention_kernel(limit_ref, qkv_ref, d_att_ref, att_ref, grads_ref):
    rows = UNIT_ROWS
    sites = rows // 2
    scale = 1.0 / math.sqrt(HEAD_DIM)
    row = lax.broadcasted_iota(jnp.int32, (rows, rows), 0)
    col = lax.broadcasted_iota(jnp.int32, (rows, rows), 1)
    upper = col >= sites
    site = jnp.where(upper, col - sites, col)
    block = upper == (row >= sites)
    masks = [
        block & (site < limit_ref[pl.program_id(0) * UNITS + unit]) for unit in range(UNITS)
    ]
    units = [(unit, head) for unit in range(UNITS) for head in range(HEAD_COLS // HEAD_DIM)]

    def part(ref, unit, head, kind):
        return ref[
            unit * rows : (unit + 1) * rows,
            kind * HEAD_COLS + head * HEAD_DIM : kind * HEAD_COLS + (head + 1) * HEAD_DIM,
        ]

    def put(ref, unit, head, kind, value):
        ref[
            unit * rows : (unit + 1) * rows,
            kind * HEAD_COLS + head * HEAD_DIM : kind * HEAD_COLS + (head + 1) * HEAD_DIM,
        ] = value.astype(jnp.bfloat16)

    scores = [
        dot(part(qkv_ref, u, h, 0), part(qkv_ref, u, h, 1), ((1,), (1,))) for u, h in units
    ]
    d_probs = [
        dot(part(d_att_ref, u, h, 0), part(qkv_ref, u, h, 2), ((1,), (1,))) for u, h in units
    ]
    low = []
    d_scores = []
    for (u, h), score, d_prob in zip(units, scores, d_probs):
        score = jnp.where(masks[u], score * scale, masked_score)
        weights = jnp.exp(score - jnp.max(score, axis=-1, keepdims=True))
        probs = weights * (1.0 / jnp.sum(weights, axis=-1, keepdims=True))
        inner = jnp.sum(probs * d_prob, axis=-1, keepdims=True)
        low.append(probs.astype(jnp.bfloat16))
        d_scores.append((probs * (d_prob - inner) * scale).astype(jnp.bfloat16))
    for (u, h), prob, d_score in zip(units, low, d_scores):
        put(att_ref, u, h, 0, dot(prob, part(qkv_ref, u, h, 2)))
        put(grads_ref, u, h, 0, dot(d_score, part(qkv_ref, u, h, 1)))
        put(grads_ref, u, h, 1, dot(d_score, part(qkv_ref, u, h, 0), ((0,), (0,))))
        put(grads_ref, u, h, 2, dot(prob, part(d_att_ref, u, h, 0), ((0,), (0,))))


def attention(limits, qkv, d_att):
    rows = UNITS * UNIT_ROWS
    count = qkv.shape[0] // rows
    spec = lambda width: pl.BlockSpec((rows, width), lambda i, limits: (i, 0))
    return pl.pallas_call(
        attention_kernel,
        grid_spec=pltpu.PrefetchScalarGridSpec(
            num_scalar_prefetch=1,
            grid=(count,),
            in_specs=[spec(3 * HEAD_COLS), spec(HEAD_COLS)],
            out_specs=[spec(HEAD_COLS), spec(3 * HEAD_COLS)],
        ),
        out_shape=[
            jax.ShapeDtypeStruct((qkv.shape[0], HEAD_COLS), jnp.bfloat16),
            jax.ShapeDtypeStruct((qkv.shape[0], 3 * HEAD_COLS), jnp.bfloat16),
        ],
        compiler_params=pltpu.CompilerParams(vmem_limit_bytes=32 * 1024 * 1024),
        cost_estimate=NO_COST,
    )(limits, qkv, d_att)


def body(
    frames,
    conv_weight,
    embed_weight,
    query_weight,
    key_weight,
    value_weight,
    output_weight,
    out_grad,
    bucket_owner,
    clip_bucket,
    clip_frames,
    clip_grid,
):
    my_dp = lax.axis_index("dp")
    my_slab = lax.axis_index("wide")
    core, y_hi = my_dp % 2, my_dp // 2
    y_lo = my_slab % 2
    heads_now = 2 * y_lo + core
    heads_across = 2 * (1 - y_lo) + core
    frame_slab = frames[0]
    clip_count, slab_frames, site_count, channels = frame_slab.shape
    width = embed_weight.shape[1]
    own_rows = clip_count * slab_frames * site_count

    def head_columns(which):
        return jnp.concatenate(
            [
                lax.dynamic_slice(w, (0, which * HEAD_COLS), (ROWS, HEAD_COLS))
                for w in (query_weight, key_weight, value_weight)
            ],
            axis=1,
        )

    x_place, z_place = (my_slab // 2) % 4, my_slab // 8
    place = jnp.where(core == 0, x_place, z_place)
    across_place = jnp.where(core == 0, z_place, x_place)
    parity = across_place % 2

    outgoing = head_columns(heads_across)
    grads, outgoing = lax.optimization_barrier((out_grad[0], outgoing))
    pair = in_order(y_lo, head_columns(heads_now), send(outgoing, Y_PARTNER))
    pair, frame_slab = lax.optimization_barrier((pair, frame_slab))
    out_pair = in_order(
        parity, send(output_weight, OUT_PAIRS[0]), send(output_weight, OUT_PAIRS[1])
    )
    first_operand = spread(jnp.concatenate([pair, out_pair], axis=2))
    embed_weight = after(embed_weight, first_operand)
    earlier = send(frame_slab, HALO)
    bucket_owner, clip_bucket, clip_frames, clip_grid = lax.optimization_barrier(
        (bucket_owner, clip_bucket, clip_frames, clip_grid, earlier)
    )[:-1]
    ring = exchange(first_operand, RINGS_FIRST)
    owners = bucket_owner[clip_bucket]
    tokens = clip_grid[..., 0] * clip_grid[..., 1]
    my_owners = owners[my_dp]
    frame_pos = my_slab * slab_frames + jnp.arange(slab_frames, dtype=jnp.int32)
    site_pos = jnp.arange(site_count, dtype=jnp.int32)
    live = (frame_pos[None, :, None] < clip_frames[my_dp][:, None, None]) & (
        site_pos[None, None, :] < tokens[my_dp][:, None, None]
    )
    group_tokens = lax.dynamic_slice(tokens, (2 * y_hi, 0), (2, clip_count)).reshape(-1)
    limits = jnp.concatenate([group_tokens, group_tokens])

    def to_group(own, *others):
        both = in_order(y_lo, own, after(send(own, Y_PARTNER), *others))
        return in_order(core, both, send(both, CORE_PARTNER), axis=1).reshape(-1, own.shape[-1])

    joined = jnp.concatenate([earlier, frame_slab], axis=1)
    active = jax.nn.silu(joined.astype(jnp.float32)).astype(jnp.bfloat16)
    summed = frame_slab.astype(jnp.float32).reshape(-1, channels)
    for offset in range(3):
        moved = active[:, slab_frames - offset : 2 * slab_frames - offset].reshape(-1, channels)
        summed = summed + dot(moved, conv_weight[offset])
    encoded = summed.astype(jnp.bfloat16)
    own_grouped = dot(encoded, embed_weight).astype(jnp.bfloat16)
    swapped = embed_weight.reshape(channels, 4, 4, -1).swapaxes(1, 2).reshape(channels, width)
    embed_now = jnp.where(core == 0, embed_weight, swapped)

    flips = [my_owners[clip] ^ my_dp for clip in range(clip_count)]
    from_owner = []
    for k in range(4):
        part = lax.dynamic_index_in_dim(grads, my_dp ^ k, 0, keepdims=False)
        part = after(part, first_operand) if k == 1 else part
        from_owner.append(part if k == 0 else send(part, DP_MOVES[k]))
    to_them = [
        jnp.where(flips[0] == k, 0, jnp.where(flips[1] == k, 1, 2)).astype(jnp.int32)
        for k in range(4)
    ]
    ring, embed_now, limits, *to_them = lax.optimization_barrier(
        (ring, embed_now, limits, *to_them)
    )
    from_owner = [after(part, ring) for part in from_owner]
    clip_up = []
    for clip in range(clip_count):
        flip = flips[clip]
        low = jnp.where(flip == 0, from_owner[0], from_owner[1])
        high = jnp.where(flip == 2, from_owner[2], from_owner[3])
        clip_up.append(jnp.where(flip < 2, low, high))
    own_up = jnp.where(live[..., None], jnp.stack(clip_up), jnp.zeros((), jnp.bfloat16))
    own_up = own_up.reshape(own_rows, width)
    second_operand, out_rows = split_ring(ring.reshape(8 * ROWS, -1))
    qkv_weight = exchange(second_operand, RINGS_SECOND).reshape(width, 3 * HEAD_COLS)

    normed = embed_and_norm(to_group(encoded, ring), embed_now)
    upstream = to_group(own_up, qkv_weight, normed)

    qkv = matmul_columns(normed, qkv_weight)
    d_attended = matmul(upstream, out_rows, (1, 1))
    attended, d_qkv = attention(limits, qkv, d_attended)

    term = terms(normed, d_qkv, attended, upstream)
    attended, term = lax.optimization_barrier((attended, term))
    by_core = attended.reshape(2, 2, own_rows, HEAD_COLS)
    rows_now, rows_across = (
        lax.dynamic_index_in_dim(by_core, which, 1, keepdims=False).reshape(-1, HEAD_COLS)
        for which in (core, 1 - core)
    )
    give_core = send(matmul(rows_across, out_rows), CORE_PARTNER)
    chip = matmul(rows_now, out_rows, add=give_core).reshape(2, own_rows, width)
    give_y = lax.dynamic_index_in_dim(chip, 1 - y_lo, 0, keepdims=False)

    keep = lax.dynamic_index_in_dim(chip, y_lo, 0, keepdims=False)
    projected = keep.astype(jnp.float32) + send(give_y, Y_PARTNER).astype(jnp.float32)
    block = (own_grouped.astype(jnp.float32) + projected).astype(jnp.bfloat16)
    block = block.reshape(clip_count, slab_frames, site_count, width)
    block = jnp.where(live[..., None], block, jnp.zeros((), jnp.bfloat16))
    block = jnp.concatenate([block, jnp.zeros_like(block[:1])])

    arrived, sent = [], []
    for k in range(4):
        part = lax.dynamic_index_in_dim(block, to_them[k], 0, keepdims=False)
        sent.append(part)
        arrived.append(part if k == 0 else send(part, DP_MOVES[k]))

    def reduced(array, groups, *others):
        return sum_parts(exchange(array, groups), *others)

    first_sum = reduced(term, RINGS_SECOND, *sent[1:])
    part = reduced(first_sum.reshape(4, 2 * ROWS, -1), RINGS_FIRST)
    part = part.reshape(2, ROWS, -1)
    part_qkv, part_out = part[..., : 3 * HEAD_COLS], part[..., 3 * HEAD_COLS :]
    even, odd = (
        lax.dynamic_index_in_dim(part_out, which, 0, keepdims=False)
        for which in (place % 2, 1 - place % 2)
    )
    came = in_order(y_lo, send(even, OUT_BACK[0]), send(odd, OUT_BACK[1]))
    mine_out = jnp.concatenate([came[0], came[1]], axis=1)
    mine_qkv = lax.dynamic_index_in_dim(part_qkv, y_lo, 0, keepdims=False)
    other_qkv = lax.dynamic_index_in_dim(part_qkv, 1 - y_lo, 0, keepdims=False)
    across = send(mine_qkv, Y_ACROSS).astype(jnp.float32)
    behind = send(other_qkv, Y_NEXT).astype(jnp.float32)
    before = send(other_qkv, Y_BEFORE).astype(jnp.float32)
    same = mine_qkv.astype(jnp.float32) + across
    cross = behind + before
    sums = jnp.concatenate([same.astype(jnp.bfloat16), cross.astype(jnp.bfloat16)], axis=1)
    across = after(send(mine_out, Y_ACROSS), sums).astype(jnp.float32)
    total_out = (mine_out.astype(jnp.float32) + across).astype(jnp.bfloat16)
    mine = jnp.concatenate([sums, total_out], axis=1)
    theirs = send(mine, CORE_PARTNER)
    grad_query, grad_key, grad_value, grad_output = final_grads(core, y_lo, mine, theirs)

    a0, a1, a2, a3 = (after(part, sums) for part in arrived)
    a0, a1 = jnp.where(core == 0, a0, a1), jnp.where(core == 0, a1, a0)
    a2, a3 = jnp.where(core == 0, a2, a3), jnp.where(core == 0, a3, a2)
    first, second = jnp.stack([a0, a1]), jnp.stack([a2, a3])
    block_out = in_order(y_hi, first, second).reshape(
        1, 4, slab_frames, site_count, width
    )
    return (block_out, grad_query, grad_key, grad_value, grad_output)


def solution(mesh):
    in_specs = (
        P("dp", None, "wide", None, None),
        P(),
        P(),
        P("wide", None),
        P("wide", None),
        P("wide", None),
        P("wide", None),
        P("dp", None, "wide", None, None),
        P(),
        P(),
        P(),
        P(),
    )
    out_specs = (
        P("dp", None, "wide", None, None),
        P("wide", None),
        P("wide", None),
        P("wide", None),
        P("wide", None),
    )
    return jax.shard_map(body, mesh=mesh, in_specs=in_specs, out_specs=out_specs, check_vma=False)
```

```python
import functools
import math

import jax
import jax.numpy as jnp
from jax import lax
from jax.experimental import pallas as pl
from jax.experimental.pallas import tpu as pltpu
from jax.sharding import PartitionSpec as P

HEAD_DIM = 128
EPS = 1e-06
masked_score = -1e30

NO_COST = pl.CostEstimate(flops=0, bytes_accessed=0, transcendentals=0)

ANYWHERE = pl.BlockSpec(memory_space=pl.ANY)

AXES = ("dp", "wide")
N_DEV = 128
N_WIDE = 32
HEAD_COLS = 384
UNIT_ROWS = 128
UNITS = 2
ROWS = 48


def place_of(index):
    dp, wide = divmod(index, N_WIDE)
    y_hi, core = divmod(dp, 2)
    z, rest = divmod(wide, 8)
    x, y_lo = divmod(rest, 2)
    return core, x, y_hi * 2 + y_lo, z


def index_of(core, x, y, z):
    y_hi, y_lo = divmod(y % 4, 2)
    return (y_hi * 2 + core % 2) * N_WIDE + (z % 4) * 8 + (x % 4) * 2 + y_lo


def pairs_by(move):
    return [(i, index_of(*move(*place_of(i)))) for i in range(N_DEV)]


Y_PARTNER = pairs_by(lambda core, x, y, z: (core, x, y ^ 1, z))
CORE_PARTNER = pairs_by(lambda core, x, y, z: (core ^ 1, x, y, z))
Y_NEXT = pairs_by(lambda core, x, y, z: (core, x, y + 1, z))
Y_BEFORE = pairs_by(lambda core, x, y, z: (core, x, y - 1, z))
Y_ACROSS = pairs_by(lambda core, x, y, z: (core, x, y + 2, z))
DP_MOVES = [[(i, i ^ (k * N_WIDE)) for i in range(N_DEV)] for k in range(4)]
HALO = [(i, i + 1) for i in range(N_DEV) if (i + 1) % N_WIDE]


def output_source(core, x, y, z, flip):
    y_hi, y_lo = divmod(y, 2)
    place, across = (z, x) if core else (x, z)
    return index_of(across // 2, place, y_hi * 2 + ((across % 2) ^ flip), 2 * y_lo + core)


RING_FLIPS = [
    pairs_by(lambda core, x, y, z, k=k: (core, x, y, z ^ k) if core else (core, x ^ k, y, z))
    for k in range(4)
]


OUT_PAIRS = [[(output_source(*place_of(i), flip), i) for i in range(N_DEV)] for flip in (0, 1)]
def spot(index):
    core, x, _, z = place_of(index)
    return z if core else x


def output_target(core, x, y, z, block):
    y_hi, y_lo = divmod(y, 2)
    place, column = (x, z) if core else (z, x)
    return index_of(column // 2, place, y_hi * 2 + block, 2 * y_lo + core)


OUT_BACK = [
    [(i, output_target(*place_of(i), block=(spot(i) % 2) ^ flip)) for i in range(N_DEV)]
    for flip in (0, 1)
]


def rings(axis_of_core):
    groups = []
    for core in range(2):
        for a in range(4):
            for y in range(4):
                if axis_of_core[core] == "z":
                    groups.append([index_of(core, a, y, z) for z in range(4)])
                else:
                    groups.append([index_of(core, x, y, a) for x in range(4)])
    return groups


RINGS_FIRST = rings("xz")
RINGS_SECOND = rings("zx")


def send(array, pairs):
    return lax.ppermute(array, AXES, pairs)


def exchange(array, groups):
    return lax.all_to_all(array, AXES, 0, 0, tiled=True, axis_index_groups=groups)


def spread(array):
    return jnp.broadcast_to(array[None], (4,) + array.shape)


def in_order(bit, mine, other, axis=0):
    return jnp.stack([jnp.where(bit == 0, mine, other), jnp.where(bit == 0, other, mine)], axis)


def after(value, *others):
    return lax.optimization_barrier((value,) + others)[0]


def embed_kernel(rows_ref, weight_ref, out_ref):
    values = dot(rows_ref[...], weight_ref[...]).astype(jnp.bfloat16)
    out_ref[...] = layer_norm(values)


def embed_and_norm(rows, weight):
    tile = 256
    return pl.pallas_call(
        embed_kernel,
        grid=(rows.shape[0] // tile,),
        in_specs=[
            pl.BlockSpec((tile, rows.shape[1]), lambda i: (i, 0)),
            pl.BlockSpec(weight.shape, lambda i: (0, 0)),
        ],
        out_specs=pl.BlockSpec((tile, weight.shape[1]), lambda i: (i, 0)),
        out_shape=jax.ShapeDtypeStruct((rows.shape[0], weight.shape[1]), jnp.bfloat16),
        compiler_params=pltpu.CompilerParams(vmem_limit_bytes=32 * 1024 * 1024),
        cost_estimate=NO_COST,
    )(rows, weight)


def layer_norm(values):
    floats = values.astype(jnp.float32)
    center = floats - jnp.mean(floats, axis=-1, keepdims=True)
    spread = jnp.mean(center * center, axis=-1, keepdims=True)
    return (center * lax.rsqrt(spread + EPS)).astype(jnp.bfloat16)


def dot(a, b, dims=((1,), (0,))):
    return lax.dot_general(a, b, (dims, ((), ())), preferred_element_type=jnp.float32)


def product_kernel(dims, added, a_ref, b_ref, *rest):
    product = dot(a_ref[...], b_ref[...], dims)
    if added:
        product = product + rest[0][...].astype(jnp.float32)
    rest[-1][...] = product.astype(jnp.bfloat16)


def matmul(a, b, dims=(1, 0), tile=256, add=None, others=()):
    rows, depth = a.shape[1 - dims[0]], a.shape[dims[0]]
    columns = b.shape[1 - dims[1]]
    if dims[0]:
        a_spec = pl.BlockSpec((tile, depth), lambda i: (i, 0))
    else:
        a_spec = pl.BlockSpec((depth, tile), lambda i: (0, i))
    out_spec = pl.BlockSpec((tile, columns), lambda i: (i, 0))
    return pl.pallas_call(
        functools.partial(product_kernel, ((dims[0],), (dims[1],)), add is not None),
        grid=(rows // tile,),
        in_specs=[a_spec, pl.BlockSpec(b.shape, lambda i: (0, 0))]
        + ([out_spec] if add is not None else [])
        + [ANYWHERE] * len(others),
        out_specs=out_spec,
        out_shape=jax.ShapeDtypeStruct((rows, columns), jnp.bfloat16),
        compiler_params=pltpu.CompilerParams(vmem_limit_bytes=40 * 1024 * 1024),
        cost_estimate=NO_COST,
    )(*((a, b) if add is None else (a, b, add)), *others)


def matmul_columns(a, b):
    rows, depth = a.shape
    return pl.pallas_call(
        functools.partial(product_kernel, ((1,), (0,)), False),
        grid=(3,),
        in_specs=[
            pl.BlockSpec((rows, depth), lambda i: (0, 0)),
            pl.BlockSpec((depth, HEAD_COLS), lambda i: (0, i)),
        ],
        out_specs=pl.BlockSpec((rows, HEAD_COLS), lambda i: (0, i)),
        out_shape=jax.ShapeDtypeStruct((rows, b.shape[1]), jnp.bfloat16),
        compiler_params=pltpu.CompilerParams(vmem_limit_bytes=40 * 1024 * 1024),
        cost_estimate=NO_COST,
    )(a, b)


def split_kernel(ring_ref, spread_ref, out_ref):
    spread_ref[0] = ring_ref[:, : 3 * HEAD_COLS]

    @pl.when(pl.program_id(0) == 0)
    def _():
        out_ref[...] = ring_ref[:, 3 * HEAD_COLS :]


def split_ring(ring):
    rows, width = ring.shape[0], ring.shape[1] - 3 * HEAD_COLS
    return pl.pallas_call(
        split_kernel,
        grid=(4,),
        in_specs=[pl.BlockSpec(ring.shape, lambda i: (0, 0))],
        out_specs=[
            pl.BlockSpec((1, rows, 3 * HEAD_COLS), lambda i: (i, 0, 0)),
            pl.BlockSpec((rows, width), lambda i: (0, 0)),
        ],
        out_shape=[
            pltpu.HBM((4, rows, 3 * HEAD_COLS), jnp.bfloat16),
            pltpu.HBM((rows, width), jnp.bfloat16),
        ],
        compiler_params=pltpu.CompilerParams(vmem_limit_bytes=32 * 1024 * 1024),
        cost_estimate=NO_COST,
    )(ring)


def term_kernel(normed_ref, d_qkv_ref, att_ref, up_ref, out_ref, total_ref):
    out_ref[0, :, : 3 * HEAD_COLS] = dot(
        normed_ref[...], d_qkv_ref[...], ((0,), (0,))
    ).astype(jnp.bfloat16)

    @pl.when(pl.program_id(0) == 0)
    def _():
        total_ref[...] = dot(att_ref[...], up_ref[...], ((0,), (0,))).astype(jnp.bfloat16)

    at = pl.multiple_of(pl.program_id(0) * 2 * ROWS, 2 * ROWS)
    for block in range(4):
        out_ref[0, block * 2 * ROWS : (block + 1) * 2 * ROWS, 3 * HEAD_COLS :] = total_ref[
            pl.ds(at, 2 * ROWS), block * HEAD_COLS : (block + 1) * HEAD_COLS
        ]


def terms(normed, d_qkv, attended, upstream):
    depth, width = normed.shape
    rows = width // 4
    whole = lambda array: pl.BlockSpec(array.shape, lambda i: (0, 0))
    return pl.pallas_call(
        term_kernel,
        grid=(4,),
        in_specs=[
            pl.BlockSpec((depth, rows), lambda i: (0, i)),
            whole(d_qkv),
            whole(attended),
            whole(upstream),
        ],
        out_specs=pl.BlockSpec((1, rows, 4 * HEAD_COLS), lambda i: (i, 0, 0)),
        out_shape=pltpu.HBM((4, rows, 4 * HEAD_COLS), jnp.bfloat16),
        scratch_shapes=[pltpu.VMEM((HEAD_COLS, width), jnp.bfloat16)],
        compiler_params=pltpu.CompilerParams(vmem_limit_bytes=40 * 1024 * 1024),
        cost_estimate=NO_COST,
    )(normed, d_qkv, attended, upstream)


def sum_kernel(parts_ref, *rest):
    out_ref = rest[-1]
    total = parts_ref[0].astype(jnp.float32)
    for i in range(1, 4):
        total = total + parts_ref[i].astype(jnp.float32)
    out_ref[...] = total.astype(jnp.bfloat16)


def sum_parts(parts, *others):
    rows, width = parts.shape[1:]
    tile = 2 * ROWS if rows > 2 * ROWS else ROWS
    return pl.pallas_call(
        sum_kernel,
        grid=(rows // tile,),
        in_specs=[pl.BlockSpec((4, tile, width), lambda i: (0, i, 0))] + [ANYWHERE] * len(others),
        out_specs=pl.BlockSpec((tile, width), lambda i: (i, 0)),
        out_shape=jax.ShapeDtypeStruct((rows, width), jnp.bfloat16),
        compiler_params=pltpu.CompilerParams(vmem_limit_bytes=32 * 1024 * 1024),
        cost_estimate=NO_COST,
    )(parts, *others)


def final_kernel(place_ref, mine_ref, theirs_ref, query_ref, key_ref, value_ref, output_ref):
    core, y_lo = place_ref[0], place_ref[1]
    wide = 3 * HEAD_COLS
    for kind, out in enumerate((query_ref, key_ref, value_ref)):
        for step in range(2):
            at = step * wide + kind * HEAD_COLS
            mine = mine_ref[:, at : at + HEAD_COLS].astype(jnp.float32)
            theirs = theirs_ref[:, at : at + HEAD_COLS].astype(jnp.float32)
            low = jnp.where(core == 0, mine, theirs)
            high = jnp.where(core == 0, theirs, mine)
            for side in range(2):

                @pl.when((y_lo ^ step) == side)
                def _():
                    begin = 2 * side * HEAD_COLS
                    out[:, begin : begin + HEAD_COLS] = low
                    out[:, begin + HEAD_COLS : begin + 2 * HEAD_COLS] = high

    mine = mine_ref[:, 2 * wide :].astype(jnp.float32)
    theirs = theirs_ref[:, 2 * wide :].astype(jnp.float32)
    output_ref[:, : 2 * HEAD_COLS] = jnp.where(core == 0, mine, theirs)
    output_ref[:, 2 * HEAD_COLS :] = jnp.where(core == 0, theirs, mine)


def final_grads(core, y_lo, mine, theirs):
    rows, width = mine.shape[0], 4 * HEAD_COLS
    whole = pl.BlockSpec(memory_space=pltpu.VMEM)
    return pl.pallas_call(
        final_kernel,
        in_specs=[pl.BlockSpec(memory_space=pltpu.SMEM), whole, whole],
        out_specs=[whole] * 4,
        out_shape=[jax.ShapeDtypeStruct((rows, width), jnp.float32)] * 4,
        cost_estimate=NO_COST,
    )(jnp.stack([core, y_lo]).astype(jnp.int32), mine, theirs)


def attention_kernel(limit_ref, qkv_ref, d_att_ref, att_ref, grads_ref):
    rows = UNIT_ROWS
    sites = rows // 2
    scale = 1.0 / math.sqrt(HEAD_DIM)
    row = lax.broadcasted_iota(jnp.int32, (rows, rows), 0)
    col = lax.broadcasted_iota(jnp.int32, (rows, rows), 1)
    upper = col >= sites
    site = jnp.where(upper, col - sites, col)
    block = upper == (row >= sites)
    masks = [
        block & (site < limit_ref[pl.program_id(0) * UNITS + unit]) for unit in range(UNITS)
    ]
    units = [(unit, head) for unit in range(UNITS) for head in range(HEAD_COLS // HEAD_DIM)]

    def part(ref, unit, head, kind):
        return ref[
            unit * rows : (unit + 1) * rows,
            kind * HEAD_COLS + head * HEAD_DIM : kind * HEAD_COLS + (head + 1) * HEAD_DIM,
        ]

    def put(ref, unit, head, kind, value):
        ref[
            unit * rows : (unit + 1) * rows,
            kind * HEAD_COLS + head * HEAD_DIM : kind * HEAD_COLS + (head + 1) * HEAD_DIM,
        ] = value.astype(jnp.bfloat16)

    scores = [
        dot(part(qkv_ref, u, h, 0), part(qkv_ref, u, h, 1), ((1,), (1,))) for u, h in units
    ]
    d_probs = [
        dot(part(d_att_ref, u, h, 0), part(qkv_ref, u, h, 2), ((1,), (1,))) for u, h in units
    ]
    low = []
    d_scores = []
    for (u, h), score, d_prob in zip(units, scores, d_probs):
        score = jnp.where(masks[u], score * scale, masked_score)
        weights = jnp.exp(score - jnp.max(score, axis=-1, keepdims=True))
        probs = weights * (1.0 / jnp.sum(weights, axis=-1, keepdims=True))
        inner = jnp.sum(probs * d_prob, axis=-1, keepdims=True)
        low.append(probs.astype(jnp.bfloat16))
        d_scores.append((probs * (d_prob - inner) * scale).astype(jnp.bfloat16))
    for (u, h), prob, d_score in zip(units, low, d_scores):
        put(att_ref, u, h, 0, dot(prob, part(qkv_ref, u, h, 2)))
        put(grads_ref, u, h, 0, dot(d_score, part(qkv_ref, u, h, 1)))
        put(grads_ref, u, h, 1, dot(d_score, part(qkv_ref, u, h, 0), ((0,), (0,))))
        put(grads_ref, u, h, 2, dot(prob, part(d_att_ref, u, h, 0), ((0,), (0,))))


def attention(limits, qkv, d_att):
    rows = UNITS * UNIT_ROWS
    count = qkv.shape[0] // rows
    spec = lambda width: pl.BlockSpec((rows, width), lambda i, limits: (i, 0))
    return pl.pallas_call(
        attention_kernel,
        grid_spec=pltpu.PrefetchScalarGridSpec(
            num_scalar_prefetch=1,
            grid=(count,),
            in_specs=[spec(3 * HEAD_COLS), spec(HEAD_COLS)],
            out_specs=[spec(HEAD_COLS), spec(3 * HEAD_COLS)],
        ),
        out_shape=[
            jax.ShapeDtypeStruct((qkv.shape[0], HEAD_COLS), jnp.bfloat16),
            jax.ShapeDtypeStruct((qkv.shape[0], 3 * HEAD_COLS), jnp.bfloat16),
        ],
        compiler_params=pltpu.CompilerParams(vmem_limit_bytes=32 * 1024 * 1024),
        cost_estimate=NO_COST,
    )(limits, qkv, d_att)


def body(
    frames,
    conv_weight,
    embed_weight,
    query_weight,
    key_weight,
    value_weight,
    output_weight,
    out_grad,
    bucket_owner,
    clip_bucket,
    clip_frames,
    clip_grid,
):
    my_dp = lax.axis_index("dp")
    my_slab = lax.axis_index("wide")
    core, y_hi = my_dp % 2, my_dp // 2
    y_lo = my_slab % 2
    heads_now = 2 * y_lo + core
    heads_across = 2 * (1 - y_lo) + core
    frame_slab = frames[0]
    clip_count, slab_frames, site_count, channels = frame_slab.shape
    width = embed_weight.shape[1]
    own_rows = clip_count * slab_frames * site_count

    def head_columns(which):
        return jnp.concatenate(
            [
                lax.dynamic_slice(w, (0, which * HEAD_COLS), (ROWS, HEAD_COLS))
                for w in (query_weight, key_weight, value_weight)
            ],
            axis=1,
        )

    x_place, z_place = (my_slab // 2) % 4, my_slab // 8
    place = jnp.where(core == 0, x_place, z_place)
    across_place = jnp.where(core == 0, z_place, x_place)
    parity = across_place % 2

    outgoing = head_columns(heads_across)
    grads, outgoing = lax.optimization_barrier((out_grad[0], outgoing))
    pair = in_order(y_lo, head_columns(heads_now), send(outgoing, Y_PARTNER))
    pair, frame_slab = lax.optimization_barrier((pair, frame_slab))
    out_pair = in_order(
        parity, send(output_weight, OUT_PAIRS[0]), send(output_weight, OUT_PAIRS[1])
    )
    first_operand = spread(jnp.concatenate([pair, out_pair], axis=2))
    embed_weight = after(embed_weight, first_operand)
    earlier = send(frame_slab, HALO)
    bucket_owner, clip_bucket, clip_frames, clip_grid = lax.optimization_barrier(
        (bucket_owner, clip_bucket, clip_frames, clip_grid, earlier)
    )[:-1]
    ring = exchange(first_operand, RINGS_FIRST)
    owners = bucket_owner[clip_bucket]
    tokens = clip_grid[..., 0] * clip_grid[..., 1]
    my_owners = owners[my_dp]
    frame_pos = my_slab * slab_frames + jnp.arange(slab_frames, dtype=jnp.int32)
    site_pos = jnp.arange(site_count, dtype=jnp.int32)
    live = (frame_pos[None, :, None] < clip_frames[my_dp][:, None, None]) & (
        site_pos[None, None, :] < tokens[my_dp][:, None, None]
    )
    group_tokens = lax.dynamic_slice(tokens, (2 * y_hi, 0), (2, clip_count)).reshape(-1)
    limits = jnp.concatenate([group_tokens, group_tokens])

    def to_group(own, *others):
        both = in_order(y_lo, own, after(send(own, Y_PARTNER), *others))
        return in_order(core, both, send(both, CORE_PARTNER), axis=1).reshape(-1, own.shape[-1])

    joined = jnp.concatenate([earlier, frame_slab], axis=1)
    active = jax.nn.silu(joined.astype(jnp.float32)).astype(jnp.bfloat16)
    summed = frame_slab.astype(jnp.float32).reshape(-1, channels)
    for offset in range(3):
        moved = active[:, slab_frames - offset : 2 * slab_frames - offset].reshape(-1, channels)
        summed = summed + dot(moved, conv_weight[offset])
    encoded = summed.astype(jnp.bfloat16)
    own_grouped = dot(encoded, embed_weight).astype(jnp.bfloat16)
    swapped = embed_weight.reshape(channels, 4, 4, -1).swapaxes(1, 2).reshape(channels, width)
    embed_now = jnp.where(core == 0, embed_weight, swapped)

    flips = [my_owners[clip] ^ my_dp for clip in range(clip_count)]
    from_owner = []
    for k in range(4):
        part = lax.dynamic_index_in_dim(grads, my_dp ^ k, 0, keepdims=False)
        part = after(part, first_operand) if k == 1 else part
        from_owner.append(part if k == 0 else send(part, DP_MOVES[k]))
    to_them = [
        jnp.where(flips[0] == k, 0, jnp.where(flips[1] == k, 1, 2)).astype(jnp.int32)
        for k in range(4)
    ]
    ring, embed_now, limits, *to_them = lax.optimization_barrier(
        (ring, embed_now, limits, *to_them)
    )
    from_owner = [after(part, ring) for part in from_owner]
    clip_up = []
    for clip in range(clip_count):
        flip = flips[clip]
        low = jnp.where(flip == 0, from_owner[0], from_owner[1])
        high = jnp.where(flip == 2, from_owner[2], from_owner[3])
        clip_up.append(jnp.where(flip < 2, low, high))
    own_up = jnp.where(live[..., None], jnp.stack(clip_up), jnp.zeros((), jnp.bfloat16))
    own_up = own_up.reshape(own_rows, width)
    second_operand, out_rows = split_ring(ring.reshape(8 * ROWS, -1))
    qkv_weight = exchange(second_operand, RINGS_SECOND).reshape(width, 3 * HEAD_COLS)

    normed = embed_and_norm(to_group(encoded, ring), embed_now)
    upstream = to_group(own_up, qkv_weight, normed)

    qkv = matmul_columns(normed, qkv_weight)
    d_attended = matmul(upstream, out_rows, (1, 1))
    attended, d_qkv = attention(limits, qkv, d_attended)

    term = terms(normed, d_qkv, attended, upstream)
    attended, term = lax.optimization_barrier((attended, term))
    by_core = attended.reshape(2, 2, own_rows, HEAD_COLS)
    rows_now, rows_across = (
        lax.dynamic_index_in_dim(by_core, which, 1, keepdims=False).reshape(-1, HEAD_COLS)
        for which in (core, 1 - core)
    )
    give_core = send(matmul(rows_across, out_rows), CORE_PARTNER)
    chip = matmul(rows_now, out_rows, add=give_core).reshape(2, own_rows, width)
    give_y = lax.dynamic_index_in_dim(chip, 1 - y_lo, 0, keepdims=False)

    keep = lax.dynamic_index_in_dim(chip, y_lo, 0, keepdims=False)
    projected = keep.astype(jnp.float32) + send(give_y, Y_PARTNER).astype(jnp.float32)
    block = (own_grouped.astype(jnp.float32) + projected).astype(jnp.bfloat16)
    block = block.reshape(clip_count, slab_frames, site_count, width)
    block = jnp.where(live[..., None], block, jnp.zeros((), jnp.bfloat16))
    block = jnp.concatenate([block, jnp.zeros_like(block[:1])])

    arrived, sent = [], []
    for k in range(4):
        part = lax.dynamic_index_in_dim(block, to_them[k], 0, keepdims=False)
        sent.append(part)
        arrived.append(part if k == 0 else send(part, DP_MOVES[k]))

    def reduced(array, groups, *others):
        return sum_parts(exchange(array, groups), *others)

    first_sum = reduced(term, RINGS_SECOND, *sent[1:])
    part = reduced(first_sum.reshape(4, 2 * ROWS, -1), RINGS_FIRST)
    part = part.reshape(2, ROWS, -1)
    part_qkv, part_out = part[..., : 3 * HEAD_COLS], part[..., 3 * HEAD_COLS :]
    even, odd = (
        lax.dynamic_index_in_dim(part_out, which, 0, keepdims=False)
        for which in (place % 2, 1 - place % 2)
    )
    came = in_order(y_lo, send(even, OUT_BACK[0]), send(odd, OUT_BACK[1]))
    mine_out = jnp.concatenate([came[0], came[1]], axis=1)
    mine_qkv = lax.dynamic_index_in_dim(part_qkv, y_lo, 0, keepdims=False)
    other_qkv = lax.dynamic_index_in_dim(part_qkv, 1 - y_lo, 0, keepdims=False)
    across = send(mine_qkv, Y_ACROSS).astype(jnp.float32)
    behind = send(other_qkv, Y_NEXT).astype(jnp.float32)
    before = send(other_qkv, Y_BEFORE).astype(jnp.float32)
    same = mine_qkv.astype(jnp.float32) + across
    cross = behind + before
    sums = jnp.concatenate([same.astype(jnp.bfloat16), cross.astype(jnp.bfloat16)], axis=1)
    across = after(send(mine_out, Y_ACROSS), sums).astype(jnp.float32)
    total_out = (mine_out.astype(jnp.float32) + across).astype(jnp.bfloat16)
    mine = jnp.concatenate([sums, total_out], axis=1)
    theirs = send(mine, CORE_PARTNER)
    grad_query, grad_key, grad_value, grad_output = final_grads(core, y_lo, mine, theirs)

    a0, a1, a2, a3 = (after(part, sums) for part in arrived)
    a0, a1 = jnp.where(core == 0, a0, a1), jnp.where(core == 0, a1, a0)
    a2, a3 = jnp.where(core == 0, a2, a3), jnp.where(core == 0, a3, a2)
    first, second = jnp.stack([a0, a1]), jnp.stack([a2, a3])
    block_out = in_order(y_hi, first, second).reshape(
        1, 4, slab_frames, site_count, width
    )
    return (block_out, grad_query, grad_key, grad_value, grad_output)


def solution(mesh):
    in_specs = (
        P("dp", None, "wide", None, None),
        P(),
        P(),
        P("wide", None),
        P("wide", None),
        P("wide", None),
        P("wide", None),
        P("dp", None, "wide", None, None),
        P(),
        P(),
        P(),
        P(),
    )
    out_specs = (
        P("dp", None, "wide", None, None),
        P("wide", None),
        P("wide", None),
        P("wide", None),
        P("wide", None),
    )
    return jax.shard_map(body, mesh=mesh, in_specs=in_specs, out_specs=out_specs, check_vma=False)
```
